32 devices in a mesh: groups: 2 (over y), dp: 8 (over z, x), mp: 2 (over core).
Axes of the slice: x: 2, y: 2, z: 4, core: 2. Of those that a mesh axis runs over, the one named last changes fastest.
Arguments:
- hidden: bfloat16 [2048, 3, 4096], P(('groups', 'dp'), None, 'mp'), parts along dimension 0, may hold values from -81 to 81
- row_owner: int32 [2048, 1], P(('groups', 'dp')), parts along dimension 0, may hold values from 0 to 7; in each aligned block of 128 rows (0 to 127, 128 to 255, ...) at most 32 rows name the same one
- candidate_shard: int32 [2048, 4], P(('groups', 'dp')), parts along dimension 0, may hold values from 0 to 7, all different within a row; in each aligned block of 128 rows (0 to 127, 128 to 255, ...) at most 96 rows name the same one
- candidate_offset: int32 [2048, 4], P(('groups', 'dp')), parts along dimension 0, may hold values from 0 to 511
- target_logits: bfloat16 [2048, 4], P(('groups', 'dp')), parts along dimension 0, may hold values from -9 to 240
- lengths: int32 [16, 4], P(('groups', 'dp')), parts along dimension 0, may hold values from 1 to 64, 128 in all within a row
- layer_mix: float32 [3, 4096], P(None, 'mp'), may hold values from 0.5 to 2
- draft_head: bfloat16 [4096, 4096], P('dp', 'mp'), may hold values from -0.09375 to 0.09375
Outputs:
- draft_logp: float32 [16, 256, 4], P(('groups', 'dp')), parts along dimension 0
- grad_mix: float32 [6, 4096], P('groups', 'mp'), parts along dimension 0
The draws below stay inside these ranges and needn't reach their ends.
There are 2 independent parts, one for each index of `groups`. The reference program is written for one: setup_inputs(seed, part) draws one part's arguments, and reference() takes and returns one part's arrays. A program takes and returns all parts, laid end to end along the dimension named above; an argument that names none is the same for every part. Nothing has to cross between parts.
Inputs may be any that keep to these rules, and one draw needn't show every extreme that they name: `row_owner`: at most 32 positions of one device have one owner. `candidate_shard`: the 4 candidates of a position lie in different shards; at most 96 candidates of one device's positions lie in one shard. The lengths of one device sum to 128.
All inputs are finite; a program needn't handle non-finite values.
Results may differ from the reference program's by a relative error of at most 0.007.
Values may be sent and summed in bfloat16 or wider, within the bound.
No kernel may reach another device: no remote copies, remote signals or barrier semaphores. Data moves between devices by JAX's collectives and lax.ppermute only.
A program may use at most 64 MiB of HBM per device.

```python
import math
import jax
import jax.numpy as jnp
import numpy as np
from jax import lax

D = 4096
VOC_DP = 512
TOPK = 4
SEQS = 4
TOK_DEV = 128
TOKENS = 1024
VOCAB = 4096
CAP = 32
CC = 96
N_DP = 8


def draw_hidden(key, part):
    key = jax.random.fold_in(key, 11)
    base_key, row_key, col_key = jax.random.split(key, 3)
    base = jnp.clip(jax.random.normal(base_key, (TOKENS, 3, D), jnp.float32), -4.0, 4.0)
    row_scale = jnp.exp(jax.random.uniform(row_key, (TOKENS, 3, 1), jnp.float32, 0.0, math.log(10.0)))
    col_scale = jnp.exp(jax.random.uniform(col_key, (1, 3, D), jnp.float32, -0.7, 0.7))
    return (base * row_scale * col_scale).astype(jnp.bfloat16)


def draw_target_logits(key, part):
    key = jax.random.fold_in(key, 23)
    base_key = jax.random.fold_in(key, 0)
    values = jnp.clip(3.0 * jax.random.normal(base_key, (TOKENS, TOPK), jnp.float32), -9.0, 9.0)
    return values.astype(jnp.bfloat16)


def set_ends(values, own_key, least, largest):
    extent = values.shape
    place = [jax.random.randint(jax.random.fold_in(own_key, axis), (), 0, extent[axis]) for axis in range(len(extent))]
    values = values.at[tuple(place)].set(least)
    longest = extent.index(max(extent))
    place[longest] = (place[longest] + 1) % extent[longest]
    return values.at[tuple(place)].set(largest)


def steps_of(stream_key, extent, pieces, low, largest):
    def one(axis_at, blocks):
        heights = jax.random.uniform(jax.random.fold_in(jax.random.fold_in(stream_key, 6), axis_at), (blocks,), jnp.float32, low / len(pieces), largest / len(pieces))
        return jnp.repeat(jnp.exp(heights), extent[axis_at] // blocks).reshape((-1,) + (1,) * (len(extent) - axis_at - 1))

    gain = one(*pieces[0])
    for cut in pieces[1:]:
        gain = gain * one(*cut)
    return gain


def split_up(amount, total, reach, skew):
    loads = [(1 << 20) // math.isqrt(grade ** skew) + 1 for grade in range(2, amount + 1)]
    surplus, counts = total - reach - (amount - 1), [1] * (amount - 1)
    while surplus > 0:
        candidates = [i for i in range(amount - 1) if counts[i] < reach]
        mass, budget = sum([loads[i] for i in candidates]), surplus
        for i in candidates:
            extra = min(reach - counts[i], max(1, budget * loads[i] // mass), surplus)
            counts[i] = counts[i] + extra
            surplus = surplus - extra
    return np.array([reach] + counts)


def ragged_sizes(rng, count, total, bound, skew):
    if count == 2:
        one = jax.random.randint(rng, (), max(1, total - bound), min(bound, total - 1) + 1)
        return jnp.stack([one, total - one])
    sizes = jnp.asarray(split_up(count, total, bound, skew), jnp.int32)
    pairs = (count - 1) // 2
    giver, sink = sizes[1:1 + 2 * pairs:2], sizes[2:2 + 2 * pairs:2]
    slack = jnp.minimum(giver - 1, bound - sink)
    moved = jax.random.randint(jax.random.fold_in(rng, 1), (pairs,), 0, 1 << 20) % (slack + 1)
    sizes = sizes.at[1:1 + 2 * pairs:2].set(giver - moved).at[2:2 + 2 * pairs:2].set(sink + moved)
    return sizes[jax.random.permutation(jax.random.fold_in(rng, 2), count)]


def assign_block(rng, own, number, rows, amount, top, limit, skew):
    ranking = jax.random.permutation(rng, amount)
    heavy_load, common = load_shares(amount, rows * top, limit, skew, True), load_shares(amount, rows * top, limit, skew, False)
    places = jnp.arange(amount)

    def named(tallies, turn):
        used = int((tallies > 0).sum())
        fixed = max(1, used // 4)
        moved = fixed + (places - fixed + turn * (used - fixed)) % max(1, amount - fixed)
        return jnp.zeros((amount,), jnp.int32).at[ranking[jnp.where(places < fixed, places, moved)]].set(jnp.asarray(tallies, jnp.int32))

    tallies = jnp.where(number % 4 == 0, named(heavy_load, number // 4), named(common, number - number // 4 - 1))
    mixed = jax.random.permutation(jax.random.fold_in(own, 3), amount)
    source_of, receiver = mixed[0:amount // 2 * 2:2], mixed[1:amount // 2 * 2:2]
    slack = jnp.minimum(tallies[source_of] - 1, limit - tallies[receiver]) // 2
    slack = jnp.where((source_of == ranking[0]) | (receiver == ranking[0]) | (tallies[receiver] == 0), 0, jnp.maximum(slack, 0))
    moved = jax.random.randint(jax.random.fold_in(own, 4), (amount // 2,), 0, 1 << 20) % (slack + 1)
    tallies = tallies.at[source_of].add(-moved).at[receiver].add(moved)
    items = jnp.searchsorted(jnp.cumsum(tallies), jnp.arange(rows * top), side="right").astype(jnp.int32)
    table = items.reshape(top, rows).T
    table = table[jax.random.permutation(jax.random.fold_in(own, 1), rows)]
    turn = jax.random.randint(jax.random.fold_in(own, 2), (rows, 1), 0, top)
    return jnp.take_along_axis(table, (jnp.arange(top)[None, :] + turn) % top, axis=1)


def load_shares(count, total, reach, skew, full):
    loads = [(1 << 20) // math.isqrt(rank ** skew) + 1 for rank in range(1, count + 1)]
    largest = reach if full else min(reach, max(-(-total // count), total * loads[0] // sum(loads)))
    least = 1 if total - largest >= count - 1 else 0
    counts, surplus = [largest] + [least] * (count - 1), total - largest - least * (count - 1)
    while surplus > 0:
        movable = [i for i in range(1, count) if counts[i] < largest] or [i for i in range(1, count) if counts[i] < reach]
        whole, left = sum([loads[i] for i in movable]), surplus
        for i in movable:
            addition = min(reach - counts[i], max(1, left * loads[i] // whole), surplus)
            counts[i] = counts[i] + addition
            surplus = surplus - addition
    return np.array(counts)


def bell_draw(key, shape, deviation, most, shards=(), held_as=jnp.bfloat16):
    result = deviation * jax.random.normal(key, shape, jnp.float32)
    if shards:
        result = result * steps_of(key, shape, shards, -0.22, 0.18)
    return jnp.clip(result, -most, most).astype(held_as)


def setup_inputs(seed: int = 0, part: int = 0) -> dict:
    streams_of = jax.random.split(jax.random.key(seed), 9)
    own_keys = jax.random.split(jax.random.fold_in(streams_of[8], part), 9)
    hidden = draw_hidden(jax.random.fold_in(jax.random.fold_in(streams_of[8], part), 71), part)
    row_owner_keys = jax.random.split(jax.random.fold_in(own_keys[1], 1), TOKENS // TOK_DEV)
    row_owner_turns = jax.random.permutation(jax.random.fold_in(own_keys[1], 3), TOKENS // TOK_DEV)
    row_owner = jax.vmap(lambda own, number: assign_block(jax.random.fold_in(own_keys[1], 2), own, number, TOK_DEV, N_DP, 1, CAP, 2))(row_owner_keys, row_owner_turns).reshape((TOKENS, 1))
    candidate_shard_keys = jax.random.split(jax.random.fold_in(own_keys[2], 1), TOKENS // TOK_DEV)
    candidate_shard_turns = jax.random.permutation(jax.random.fold_in(own_keys[2], 3), TOKENS // TOK_DEV)
    candidate_shard = jax.vmap(lambda own, number: assign_block(jax.random.fold_in(own_keys[2], 2), own, number, TOK_DEV, N_DP, TOPK, CC, 2))(candidate_shard_keys, candidate_shard_turns).reshape((TOKENS, TOPK))
    candidate_offset = set_ends(jax.random.randint(own_keys[3], (TOKENS, TOPK), 0, VOC_DP), jax.random.fold_in(own_keys[3], 1), 0, VOC_DP - 1).astype(jnp.int32)
    target_logits = draw_target_logits(jax.random.fold_in(jax.random.fold_in(streams_of[8], part), 71), part)
    lengths = jax.vmap(lambda own: ragged_sizes(own, SEQS, TOK_DEV, TOK_DEV // 2, 2))(jax.random.split(own_keys[5], N_DP)).reshape((N_DP, SEQS)).astype(jnp.int32)
    layer_mix = jnp.clip(jnp.exp(math.log(2.0) - 1.3862944 * jax.random.uniform(streams_of[6], (3, D), jnp.float32) ** steps_of(streams_of[6], (3, D), ((1, 2),), -0.2, 0.2)), 0.5, 2.0)
    draft_head = bell_draw(streams_of[7], (VOCAB, D), D ** -0.5, 0.09375, ((0, 8), (1, 2)))
    return {"hidden": hidden, "row_owner": row_owner, "candidate_shard": candidate_shard, "candidate_offset": candidate_offset, "target_logits": target_logits, "lengths": lengths, "layer_mix": layer_mix, "draft_head": draft_head}


EPS = 1e-06
HIGHEST = lax.Precision.HIGHEST

def slot_ranks(target, number):
    one_hot = (target[:, None] == jnp.arange(number, dtype=jnp.int32)[None, :]).astype(jnp.int32)
    before = jnp.cumsum(one_hot, axis=0) - one_hot
    return lax.optimization_barrier(jnp.sum(before * one_hot, axis=1)).astype(jnp.int32)

def position_weights(lengths, positions, sequences):
    seq_ends = jnp.cumsum(lengths)
    seq_starts = seq_ends - lengths
    position = jnp.arange(positions, dtype=jnp.int32)[:, None]
    member = (position >= seq_starts[None, :]) & (position < seq_ends[None, :])
    own_length = lax.optimization_barrier(jnp.sum(jnp.where(member, lengths[None, :], 0), axis=1))
    closing = jnp.any(member & (position == seq_ends[None, :] - 1), axis=1)
    portion = 1.0 / (own_length.astype(jnp.float32) * sequences)
    return jnp.where(closing, 0.0, portion).astype(jnp.bfloat16)

def device_terms(tokens, head_rows, target_logits, weight, layer_mix):
    wide_tokens = tokens.astype(jnp.float32)
    wide_heads = head_rows.astype(jnp.float32)
    partial_value = jnp.einsum('rlf,rkf->rkl', wide_tokens * layer_mix[None], wide_heads, precision=HIGHEST)
    squares = lax.optimization_barrier(jnp.sum(wide_tokens * wide_tokens, axis=2))
    inverse = lax.rsqrt(squares / D + EPS)
    logits = jnp.einsum('rkl,rl->rk', partial_value, inverse, precision=HIGHEST)
    draft_logp = jax.nn.log_softmax(logits, axis=1)
    target = jax.nn.softmax(target_logits.astype(jnp.float32), axis=1)
    grad_logits = weight.astype(jnp.float32)[:, None] * (jnp.exp(draft_logp) - target)
    carried = jnp.einsum('rk,rkf->rf', grad_logits, wide_heads, precision=HIGHEST)
    gradient = jnp.einsum('rlf,rl,rf->lf', wide_tokens, inverse, carried, precision=HIGHEST)
    return (draft_logp, gradient)

def reference(hidden, row_owner, candidate_shard, candidate_offset, target_logits, lengths, layer_mix, draft_head):
    device_hidden = hidden.reshape(N_DP, TOK_DEV, 3, D)
    device_shard = candidate_shard.reshape(N_DP, TOK_DEV, TOPK)
    device_offset = candidate_offset.reshape(N_DP, TOK_DEV, TOPK)
    device_logits = target_logits.reshape(N_DP, TOK_DEV, TOPK)

    def one_device(grad_total, device_block):
        tokens, shard, offset, logits_in, device_lengths = device_block
        ids = (shard * VOC_DP + offset).reshape(-1).astype(jnp.int32)
        head_rows = jnp.take(draft_head, ids, axis=0).reshape(TOK_DEV, TOPK, D)
        weight = position_weights(device_lengths, TOK_DEV, float(SEQS * N_DP))
        draft_logp, gradient = device_terms(tokens, head_rows, logits_in, weight, layer_mix)
        return (grad_total + gradient, draft_logp)
    grad_mix, logp_all = lax.scan(one_device, jnp.zeros((3, D), jnp.float32), (device_hidden, device_shard, device_offset, device_logits, lengths))
    owner_ids = row_owner.reshape(N_DP, TOK_DEV).astype(jnp.int32)

    def device_ranks(owners_here):
        return slot_ranks(owners_here, N_DP)
    owner_rank = jax.vmap(device_ranks)(owner_ids)
    source = jnp.broadcast_to(jnp.arange(N_DP, dtype=jnp.int32)[:, None], (N_DP, TOK_DEV))
    slots = jnp.zeros((N_DP, N_DP, CAP, TOPK), jnp.float32).at[owner_ids, source, owner_rank].set(logp_all)
    return (slots.reshape(N_DP, N_DP * CAP, TOPK), grad_mix)
```

```python
import functools

import jax
import jax.numpy as jnp
from jax import lax
from jax.experimental import pallas as pl
from jax.experimental.pallas import tpu as pltpu
from jax.sharding import PartitionSpec as P

EPS = 1e-06
HIGHEST = lax.Precision.HIGHEST
F32 = jnp.float32
BF16 = jnp.bfloat16
VMEM_LIMIT = 48 * 1024 * 1024


def iota(shape, axis):
    return lax.broadcasted_iota(jnp.int32, shape, axis)


def slot_mask(asked, spread):
    shards, rows = asked.shape
    held = asked >= 0
    earlier = (iota((rows, rows), 0) < iota((rows, rows), 1)).astype(BF16)
    rank = jnp.dot(held.astype(BF16), earlier, preferred_element_type=F32)
    rank = jnp.where(held, rank, -1.0)
    place = iota((shards, spread, rows), 1).astype(F32)
    return rank[:, None, :] == place


def pick_kernel(asked_ref, head_ref, out_ref, hot_ref, *, spread):
    @pl.when(pl.program_id(0) == 0)
    def _():
        asked = asked_ref[...]
        shards, rows = asked.shape
        mask = slot_mask(asked, spread)
        row = jnp.where(mask, (asked.astype(F32) + 1.0)[:, None, :], 0.0)
        row = jnp.sum(row.reshape(shards * spread, rows), axis=1, keepdims=True) - 1.0
        lane = iota((1, head_ref.shape[0]), 1).astype(F32)
        hot_ref[...] = jnp.where(row == lane, 1.0, 0.0).astype(BF16)

    out_ref[...] = jnp.dot(hot_ref[...], head_ref[...], preferred_element_type=F32).astype(BF16)


def score_kernel(asked_ref, mixed_ref, rows_ref, out_ref, total_ref, *, spread):
    step = pl.program_id(0)

    @pl.when(step == 0)
    def _():
        total_ref[...] = jnp.zeros_like(total_ref)

    total_ref[...] += lax.dot_general(
        rows_ref[...], mixed_ref[...], (((1,), (1,)), ((), ())), preferred_element_type=F32
    )

    @pl.when(step == pl.num_programs(0) - 1)
    def _():
        asked = asked_ref[...]
        shards, rows = asked.shape
        score = total_ref[:, :rows] + total_ref[:, rows:]
        mask = slot_mask(asked, spread)
        out_ref[...] = jnp.sum(
            jnp.where(mask, score.reshape(shards, spread, rows), 0.0), axis=1
        )


def grad_kernel(
    own_ref,
    other_ref,
    asked_ref,
    shard_ref,
    target_ref,
    weight_ref,
    slot_ref,
    inverse_ref,
    rows_ref,
    hidden_ref,
    sent_ref,
    grad_ref,
    part_ref,
    *,
    spread,
):
    @pl.when(pl.program_id(0) == 0)
    def _():
        asked = asked_ref[...]
        shards, rows = asked.shape
        top = shard_ref.shape[0]
        shard = shard_ref[...]
        by_shard = own_ref[...] + other_ref[...]
        number = iota((shards, rows), 0)
        logits = jnp.concatenate(
            [
                jnp.sum(jnp.where(shard[k : k + 1] == number, by_shard, 0.0), axis=0, keepdims=True)
                for k in range(top)
            ],
            axis=0,
        )
        logits = logits - jnp.max(logits, axis=0, keepdims=True)
        logp = logits - jnp.log(jnp.sum(jnp.exp(logits), axis=0, keepdims=True))
        grad = weight_ref[...] * (jnp.exp(logp) - target_ref[...])
        by_shard = jnp.zeros((shards, rows), F32)
        for k in range(top):
            by_shard = jnp.where(shard[k : k + 1] == number, grad[k : k + 1], by_shard)
        part = jnp.where(slot_mask(asked, spread), by_shard[:, None, :], 0.0)
        part_ref[...] = part.reshape(shards * spread, rows).astype(BF16)
        slots = sent_ref.shape[1]
        placed = (iota((slots, rows), 0) == slot_ref[...]).astype(F32)
        sent_ref[...] = lax.dot_general(
            logp, placed, (((1,), (1,)), ((), ())), preferred_element_type=F32, precision=HIGHEST
        )

    carried = lax.dot_general(
        part_ref[...], rows_ref[...], (((0,), (0,)), ((), ())), preferred_element_type=F32
    )
    for layer in range(hidden_ref.shape[0]):
        scaled = hidden_ref[layer].astype(F32) * inverse_ref[:, layer : layer + 1]
        grad_ref[layer : layer + 1, :] = jnp.sum(scaled * carried, axis=0, keepdims=True)


def whole(shape):
    return pl.BlockSpec(shape, lambda i: (0,) * len(shape))


def params():
    return pltpu.CompilerParams(vmem_limit_bytes=VMEM_LIMIT)


def block_of(features):
    return 512 if features % 512 == 0 else features


def pick(asked, head, spread):
    rows, features = head.shape
    slots, wide = asked.shape[0] * spread, block_of(features)
    return pl.pallas_call(
        functools.partial(pick_kernel, spread=spread),
        grid=(features // wide,),
        in_specs=[whole(asked.shape), pl.BlockSpec((rows, wide), lambda i: (0, i))],
        out_specs=pl.BlockSpec((slots, wide), lambda i: (0, i)),
        out_shape=jax.ShapeDtypeStruct((slots, features), BF16),
        scratch_shapes=[pltpu.VMEM((slots, rows), BF16)],
        compiler_params=params(),
        name="pick",
    )(asked, head)


def score(asked, mixed, fetched, spread):
    slots, features = fetched.shape
    wide = block_of(features)
    return pl.pallas_call(
        functools.partial(score_kernel, spread=spread),
        grid=(features // wide,),
        in_specs=[
            whole(asked.shape),
            pl.BlockSpec((mixed.shape[0], wide), lambda i: (0, i)),
            pl.BlockSpec((slots, wide), lambda i: (0, i)),
        ],
        out_specs=whole(asked.shape),
        out_shape=jax.ShapeDtypeStruct(asked.shape, F32),
        scratch_shapes=[pltpu.VMEM((slots, mixed.shape[0]), F32)],
        compiler_params=params(),
        name="score",
    )(asked, mixed, fetched)


def gradient(own, other, asked, shard, target, weight, slot, inverse, fetched, hidden, spread, slots):
    features = fetched.shape[1]
    wide = block_of(features)
    layers, rows = hidden.shape[:2]
    return pl.pallas_call(
        functools.partial(grad_kernel, spread=spread),
        grid=(features // wide,),
        in_specs=[
            whole(a.shape) for a in (own, other, asked, shard, target, weight, slot, inverse)
        ]
        + [
            pl.BlockSpec((fetched.shape[0], wide), lambda i: (0, i)),
            pl.BlockSpec((layers, rows, wide), lambda i: (0, 0, i)),
        ],
        out_specs=[
            whole((shard.shape[0], slots)),
            pl.BlockSpec((layers, wide), lambda i: (0, i)),
        ],
        out_shape=[
            jax.ShapeDtypeStruct((shard.shape[0], slots), F32),
            jax.ShapeDtypeStruct((layers, features), F32),
        ],
        scratch_shapes=[pltpu.VMEM((fetched.shape[0], rows), BF16)],
        compiler_params=params(),
        name="gradient",
    )(own, other, asked, shard, target, weight, slot, inverse, fetched, hidden)


def position_weights(lengths, positions, sequences):
    seq_ends = jnp.cumsum(lengths)
    seq_starts = seq_ends - lengths
    position = jnp.arange(positions, dtype=jnp.int32)[None, :]
    member = (position >= seq_starts[:, None]) & (position < seq_ends[:, None])
    own_length = jnp.sum(jnp.where(member, lengths[:, None], 0), axis=0, keepdims=True)
    closing = jnp.any(member & (position == seq_ends[:, None] - 1), axis=0, keepdims=True)
    portion = 1.0 / (own_length.astype(F32) * sequences)
    return jnp.where(closing, 0.0, portion).astype(BF16).astype(F32)


def swap_cores(value):
    size = lax.axis_size("mp")
    if size == 1:
        return jnp.zeros_like(value)
    return lax.ppermute(value, "mp", [(i, i ^ 1) for i in range(size)])


def sum_over(value, axis):
    size = lax.axis_size(axis)
    if size & (size - 1) or size > 16:
        return lax.psum(value, axis)
    step = 1
    while step < size:
        value = value + lax.ppermute(value, axis, [(i, i ^ step) for i in range(size)])
        step *= 2
    return value


def exchange(value):
    return lax.all_to_all(value, "dp", split_axis=0, concat_axis=0, tiled=True)


def local(
    hidden,
    row_owner,
    candidate_shard,
    candidate_offset,
    target_logits,
    lengths,
    layer_mix,
    draft_head,
):
    rows, layers, features = hidden.shape
    top = candidate_shard.shape[1]
    peers = lax.axis_size("dp")
    cores = lax.axis_size("mp")
    capacity = max(2, 2 * rows // peers)
    spread = min(rows, max(2, 3 * rows * top // (2 * peers)))
    spread = -(-spread // 8) * 8

    shard = candidate_shard.T
    offset = candidate_offset.T
    number = jnp.arange(peers, dtype=jnp.int32)[:, None]
    asked = jnp.max(
        jnp.where(shard[:, None, :] == number[None], offset[:, None, :], -1), axis=0
    )
    picked = pick(exchange(asked), draft_head, spread)
    fetched = exchange(picked.reshape(peers, spread, features)).reshape(peers * spread, features)

    tokens = hidden.transpose(1, 0, 2)
    wide = tokens.astype(F32)
    squares = jnp.sum(wide * wide, axis=2)
    squares = squares + swap_cores(squares)
    inverse = lax.rsqrt(squares / (features * cores) + EPS)
    mixed = jnp.sum(wide * layer_mix[:, None, :] * inverse[:, :, None], axis=0)
    high = mixed.astype(BF16)
    low = (mixed - high.astype(F32)).astype(BF16)
    mixed = jnp.concatenate([high, low], axis=0)

    weight = position_weights(lengths[0], rows, float(lengths.shape[1] * peers))
    target = jax.nn.softmax(target_logits.T.astype(F32), axis=0)
    owner = row_owner.T
    same = (owner.T == owner) & (iota((rows, rows), 1) < iota((rows, rows), 0))
    slot = owner * capacity + jnp.sum(same.astype(jnp.int32), axis=1)[None, :]

    own = score(asked, mixed, fetched, spread)
    sent, grad = gradient(
        own,
        swap_cores(own),
        asked,
        shard,
        target,
        weight,
        slot,
        inverse.T,
        fetched,
        tokens,
        spread,
        peers * capacity,
    )
    sent = sent.reshape(top, peers, capacity).transpose(1, 0, 2)
    draft_logp = exchange(sent).transpose(0, 2, 1).reshape(1, peers * capacity, top)
    return (draft_logp, sum_over(grad, "dp"))


def solution(mesh):
    return jax.shard_map(
        local,
        mesh=mesh,
        in_specs=(
            P(("groups", "dp"), None, "mp"),
            P(("groups", "dp"), None),
            P(("groups", "dp"), None),
            P(("groups", "dp"), None),
            P(("groups", "dp"), None),
            P(("groups", "dp"), None),
            P(None, "mp"),
            P("dp", "mp"),
        ),
        out_specs=(P(("groups", "dp"), None, None), P("groups", "mp")),
        check_vma=False,
    )
```

```python
import functools

import jax
import jax.numpy as jnp
from jax import lax
from jax.experimental import pallas as pl
from jax.experimental.pallas import tpu as pltpu
from jax.sharding import PartitionSpec as P

EPS = 1e-06
HIGHEST = lax.Precision.HIGHEST
F32 = jnp.float32
BF16 = jnp.bfloat16
VMEM_LIMIT = 40 * 1024 * 1024


def iota(shape, axis):
    return lax.broadcasted_iota(jnp.int32, shape, axis)


def slot_mask(asked, spread):
    shards, rows = asked.shape
    held = asked >= 0
    earlier = (iota((rows, rows), 0) < iota((rows, rows), 1)).astype(BF16)
    rank = jnp.dot(held.astype(BF16), earlier, preferred_element_type=F32)
    rank = jnp.where(held, rank, -1.0)
    place = iota((shards, spread, rows), 1).astype(F32)
    return rank[:, None, :] == place


def pieces(features):
    wide = 512 if features % 512 == 0 else features
    return [pl.ds(start, wide) for start in range(0, features, wide)]


def fetch(source, target, sems):
    lead = (slice(None),) * (len(source.shape) - 1)
    copies = [
        pltpu.make_async_copy(source.at[(*lead, cut)], target.at[(*lead, cut)], sems.at[i])
        for i, cut in enumerate(pieces(source.shape[-1]))
    ]
    for copy in copies:
        copy.start()
    return copies


def pick_kernel(asked_ref, head_hbm, out_hbm, head_ref, picked_ref, in_sems, out_sems, *, spread):
    arrivals = fetch(head_hbm, head_ref, in_sems)
    asked = asked_ref[...]
    shards, rows = asked.shape
    mask = slot_mask(asked, spread)
    row = jnp.where(mask, (asked.astype(F32) + 1.0)[:, None, :], 0.0)
    row = jnp.sum(row.reshape(shards * spread, rows), axis=1, keepdims=True) - 1.0
    lane = iota((1, head_ref.shape[0]), 1).astype(F32)
    hot = jnp.where(row == lane, 1.0, 0.0).astype(BF16)
    departures = []
    for i, cut in enumerate(pieces(head_ref.shape[1])):
        arrivals[i].wait()
        picked_ref[:, cut] = jnp.dot(
            hot, head_ref[:, cut], preferred_element_type=F32
        ).astype(BF16)
        copy = pltpu.make_async_copy(picked_ref.at[:, cut], out_hbm.at[:, cut], out_sems.at[i])
        copy.start()
        departures.append(copy)
    for copy in departures:
        copy.wait()


def score_kernel(pack_ref, mixed_hbm, rows_ref, out_ref, mask_ref, mixed_ref, sems):
    arrivals = fetch(mixed_hbm, mixed_ref, sems)
    shards, rows = out_ref.shape
    spread = rows_ref.shape[0] // shards
    mask = slot_mask(pack_ref[:shards, :], spread).astype(F32)
    mask_ref[...] = mask.reshape(mask_ref.shape).astype(BF16)
    for copy in arrivals:
        copy.wait()
    score = lax.dot_general(
        rows_ref[...], mixed_ref[...], (((1,), (1,)), ((), ())), preferred_element_type=F32
    )
    score = (score[:, :rows] + score[:, rows:]).reshape(mask.shape)
    out_ref[...] = jnp.sum(score * mask, axis=1)


def grad_kernel(
    own_ref,
    other_ref,
    pack_ref,
    mask_ref,
    rows_ref,
    hidden_hbm,
    out_ref,
    hidden_ref,
    grad_ref,
    sems,
    *,
    top,
):
    arrivals = fetch(hidden_hbm, hidden_ref, sems)
    layers, rows, features = hidden_ref.shape
    shards = own_ref.shape[0]
    lines = grad_ref.shape[0]
    slots = 128 * ((out_ref.shape[1] - lines) // (2 * top))
    pack = pack_ref[shards:, :]
    shard, target = pack[:top], pack[top : 2 * top]
    weight, owner, column = [pack[2 * top + i : 2 * top + i + 1] for i in range(3)]
    inverse = pack[2 * top + 3 :].T

    by_shard = own_ref[...] + other_ref[...]
    number = iota((shards, rows), 0).astype(F32)
    logits = jnp.concatenate(
        [
            jnp.sum(jnp.where(shard[k : k + 1] == number, by_shard, 0.0), axis=0, keepdims=True)
            for k in range(top)
        ],
        axis=0,
    )
    logits = logits - jnp.max(logits, axis=0, keepdims=True)
    logp = logits - jnp.log(jnp.sum(jnp.exp(logits), axis=0, keepdims=True))
    grad = weight * (jnp.exp(logp) - target)
    by_shard = jnp.zeros((shards, rows), F32)
    for k in range(top):
        by_shard = jnp.where(shard[k : k + 1] == number, grad[k : k + 1], by_shard)
    mask = mask_ref[...].astype(F32).reshape(shards, mask_ref.shape[0] // shards, rows)
    part = (mask * by_shard[:, None, :]).reshape(mask_ref.shape).astype(BF16)

    for i, cut in enumerate(pieces(features)):
        carried = lax.dot_general(
            part, rows_ref[:, cut], (((0,), (0,)), ((), ())), preferred_element_type=F32
        )
        arrivals[i].wait()
        wide = carried.shape[1]
        for layer in range(layers):
            scaled = hidden_ref[layer, :, cut].astype(F32) * inverse[:, layer : layer + 1]
            total = jnp.sum(scaled * carried, axis=0, keepdims=True)
            for j in range(wide // 128):
                line = layer * (features // 128) + i * (wide // 128) + j
                grad_ref[line : line + 1, :] = total[:, j * 128 : (j + 1) * 128]

    high = logp.astype(BF16).astype(F32)
    halves = jnp.concatenate([high, logp - high], axis=0)
    owned = jnp.where(owner == iota((shards, 1, rows), 0).astype(F32), halves[None], 0.0)
    owned = owned.reshape(shards * 2 * top, rows).astype(BF16)
    placed = (iota((slots, rows), 0).astype(F32) == column).astype(BF16)
    sent = lax.dot_general(owned, placed, (((1,), (1,)), ((), ())), preferred_element_type=F32)
    sent = [
        sent[:, j * 128 : (j + 1) * 128].reshape(shards, 2 * top, 128) for j in range(slots // 128)
    ]
    out_ref[:, lines:, :] = jnp.concatenate(sent, axis=1).astype(BF16)
    grad = grad_ref[...].astype(BF16)
    for peer in range(shards):
        out_ref[peer, 0:lines, :] = grad


def sum_kernel(parts_ref, grad_ref, logp_ref):
    total = parts_ref[0].astype(F32)
    for peer in range(1, parts_ref.shape[0]):
        total = total + parts_ref[peer].astype(F32)
    layers, features = grad_ref.shape
    top, slots = logp_ref.shape
    each = features // 128
    for layer in range(layers):
        for j in range(each):
            line = layer * each + j
            grad_ref[layer : layer + 1, j * 128 : (j + 1) * 128] = total[line : line + 1]
    for j in range(slots // 128):
        first = layers * each + j * 2 * top
        logp_ref[:, j * 128 : (j + 1) * 128] = (
            total[first : first + top] + total[first + top : first + 2 * top]
        )


VMEM = pl.BlockSpec(memory_space=pltpu.VMEM)
HBM = pl.BlockSpec(memory_space=pltpu.HBM)


def params():
    return pltpu.CompilerParams(vmem_limit_bytes=VMEM_LIMIT)


def in_hbm(value):
    return pltpu.with_memory_space_constraint(value, pltpu.HBM)


def pick(asked, head, spread):
    rows, features = head.shape
    slots, count = asked.shape[0] * spread, len(pieces(features))
    return pl.pallas_call(
        functools.partial(pick_kernel, spread=spread),
        in_specs=[VMEM, HBM],
        out_specs=HBM,
        out_shape=pltpu.HBM((slots, features), BF16),
        scratch_shapes=[
            pltpu.VMEM((rows, features), BF16),
            pltpu.VMEM((slots, features), BF16),
            pltpu.SemaphoreType.DMA((count,)),
            pltpu.SemaphoreType.DMA((count,)),
        ],
        compiler_params=params(),
        name="pick",
    )(asked, in_hbm(head))


def score(pack, mixed, fetched, shards):
    rows = pack.shape[1]
    return pl.pallas_call(
        score_kernel,
        in_specs=[VMEM, HBM, VMEM],
        out_specs=[VMEM, VMEM],
        out_shape=[
            jax.ShapeDtypeStruct((shards, rows), F32),
            jax.ShapeDtypeStruct((fetched.shape[0], rows), BF16),
        ],
        scratch_shapes=[
            pltpu.VMEM(mixed.shape, BF16),
            pltpu.SemaphoreType.DMA((len(pieces(mixed.shape[1])),)),
        ],
        compiler_params=params(),
        name="score",
    )(pack, in_hbm(mixed), fetched)


def gradient(own, other, pack, mask, fetched, hidden, lines, total_lines, top):
    count = len(pieces(hidden.shape[2]))
    return pl.pallas_call(
        functools.partial(grad_kernel, top=top),
        in_specs=[VMEM] * 5 + [HBM],
        out_specs=VMEM,
        out_shape=jax.ShapeDtypeStruct((own.shape[0], total_lines, 128), BF16),
        scratch_shapes=[
            pltpu.VMEM(hidden.shape, BF16),
            pltpu.VMEM((lines, 128), F32),
            pltpu.SemaphoreType.DMA((count,)),
        ],
        compiler_params=params(),
        name="gradient",
    )(own, other, pack, mask, fetched, in_hbm(hidden))


def add_up(parts, layers, features, top, slots):
    return pl.pallas_call(
        sum_kernel,
        in_specs=[VMEM],
        out_specs=[VMEM] * 2,
        out_shape=[
            jax.ShapeDtypeStruct((layers, features), F32),
            jax.ShapeDtypeStruct((top, slots), F32),
        ],
        compiler_params=params(),
        name="add_up",
    )(parts)


def rounded(value):
    return lax.reduce_precision(value, exponent_bits=8, mantissa_bits=7)


def position_weights(lengths, positions, sequences):
    seq_ends = jnp.cumsum(lengths)
    seq_starts = seq_ends - lengths
    position = jnp.arange(positions, dtype=jnp.int32)[None, :]
    member = (position >= seq_starts[:, None]) & (position < seq_ends[:, None])
    own_length = jnp.sum(jnp.where(member, lengths[:, None], 0), axis=0, keepdims=True)
    closing = jnp.any(member & (position == seq_ends[:, None] - 1), axis=0, keepdims=True)
    portion = 1.0 / (own_length.astype(F32) * sequences)
    return rounded(jnp.where(closing, 0.0, portion))


def swap_cores(value):
    size = lax.axis_size("mp")
    if size == 1:
        return jnp.zeros_like(value)
    return lax.ppermute(value, "mp", [(i, i ^ 1) for i in range(size)])


def exchange(value):
    return lax.all_to_all(value, "dp", split_axis=0, concat_axis=0, tiled=True)


def local(
    hidden,
    row_owner,
    candidate_shard,
    candidate_offset,
    target_logits,
    lengths,
    layer_mix,
    draft_head,
):
    rows, layers, features = hidden.shape
    top = candidate_shard.shape[1]
    peers = lax.axis_size("dp")
    cores = lax.axis_size("mp")
    capacity = max(2, 2 * rows // peers)
    spread = min(rows, max(2, 3 * rows * top // (2 * peers)))
    spread = -(-spread // 8) * 8

    shard = candidate_shard.T
    offset = candidate_offset.T
    number = jnp.arange(peers, dtype=jnp.int32)[:, None]
    asked = jnp.max(
        jnp.where(shard[:, None, :] == number[None], offset[:, None, :], -1), axis=0
    )
    picked = pick(exchange(asked), draft_head, spread)
    fetched = exchange(picked.reshape(peers, spread, features)).reshape(peers * spread, features)

    tokens = hidden.transpose(1, 0, 2)
    wide = tokens.astype(F32)
    squares = jnp.sum(wide * wide, axis=2)
    squares = squares + swap_cores(squares)
    inverse = lax.rsqrt(squares / (features * cores) + EPS)
    mixed = jnp.sum(wide * layer_mix[:, None, :] * inverse[:, :, None], axis=0)
    high = rounded(mixed)
    mixed = jnp.concatenate([high, mixed - high], axis=0).astype(BF16)

    weight = position_weights(lengths[0], rows, float(lengths.shape[1] * peers))
    target = jax.nn.softmax(target_logits.T.astype(F32), axis=0)
    owner = row_owner.T
    same = (owner.T == owner) & (iota((rows, rows), 1) < iota((rows, rows), 0))
    column = lax.axis_index("dp") * capacity + jnp.sum(same.astype(jnp.int32), axis=1)[None, :]
    pack = [asked, shard, target, weight, owner, column, inverse]
    pack = jnp.concatenate([value.astype(F32) for value in pack], axis=0)
    pack = jnp.pad(pack, ((0, -pack.shape[0] % 8), (0, 0)))

    slots = peers * capacity
    lines = layers * features // 128
    total_lines = lines + 2 * top * slots // 128
    own, mask = score(pack, mixed, fetched, peers)
    parts = gradient(own, swap_cores(own), pack, mask, fetched, tokens, lines, total_lines, top)
    grad, logp = add_up(exchange(parts), layers, features, top, slots)
    return (logp.T[None], grad)


def solution(mesh):
    return jax.shard_map(
        local,
        mesh=mesh,
        in_specs=(
            P(("groups", "dp"), None, "mp"),
            P(("groups", "dp"), None),
            P(("groups", "dp"), None),
            P(("groups", "dp"), None),
            P(("groups", "dp"), None),
            P(("groups", "dp"), None),
            P(None, "mp"),
            P("dp", "mp"),
        ),
        out_specs=(P(("groups", "dp"), None, None), P("groups", "mp")),
        check_vma=False,
    )
```

```python
import functools

import jax
import jax.numpy as jnp
from jax import lax
from jax.experimental import pallas as pl
from jax.experimental.pallas import tpu as pltpu
from jax.sharding import PartitionSpec as P

EPS = 1e-06
HIGHEST = lax.Precision.HIGHEST
F32 = jnp.float32
BF16 = jnp.bfloat16
VMEM_LIMIT = 40 * 1024 * 1024
CHUNKS = (256, 256)


def iota(shape, axis):
    return lax.broadcasted_iota(jnp.int32, shape, axis)


def slot_mask(asked, spread):
    shards, rows = asked.shape
    held = asked >= 0
    earlier = (iota((rows, rows), 0) < iota((rows, rows), 1)).astype(BF16)
    rank = jnp.dot(held.astype(BF16), earlier, preferred_element_type=F32)
    rank = jnp.where(held, rank, -1.0)
    place = iota((shards, spread, rows), 1).astype(F32)
    return rank[:, None, :] == place


def pieces(features):
    return [pl.ds(start, min(512, features - start)) for start in range(0, features, 512)]


def fetch(source, target, sems):
    lead = (slice(None),) * (len(source.shape) - 1)
    copies = [
        pltpu.make_async_copy(source.at[(*lead, cut)], target.at[(*lead, cut)], sems.at[i])
        for i, cut in enumerate(pieces(source.shape[-1]))
    ]
    for copy in copies:
        copy.start()
    return copies


def hot_rows(asked, spread, count):
    shards, rows = asked.shape
    mask = slot_mask(asked, spread)
    row = jnp.where(mask, (asked.astype(F32) + 1.0)[:, None, :], 0.0)
    row = jnp.sum(row.reshape(shards * spread, rows), axis=1, keepdims=True) - 1.0
    return jnp.where(row == iota((1, count), 1).astype(F32), 1.0, 0.0).astype(BF16)


def every_other(ref, first):
    lines = [ref[i : i + 1, :] for i in range(first, ref.shape[0], 2)]
    return jnp.concatenate(lines, axis=0)


def pick_kernel(asked_ref, head_hbm, out_hbm, head_ref, picked_ref, in_sems, out_sems, *, spread):
    late = head_ref.shape[1]
    arrivals = fetch(head_hbm.at[:, :late], head_ref, in_sems)
    hot = hot_rows(every_other(asked_ref, 0), spread, head_ref.shape[0])
    departures = []
    for i, cut in enumerate(pieces(late)):
        arrivals[i].wait()
        picked_ref[:, cut] = jnp.dot(
            hot, head_ref[:, cut], preferred_element_type=F32
        ).astype(BF16)
        copy = pltpu.make_async_copy(picked_ref.at[:, cut], out_hbm.at[:, cut], out_sems.at[i])
        copy.start()
        departures.append(copy)
    for copy in departures:
        copy.wait()


def early_kernel(asked_ref, head_hbm, near_hbm, far_hbm, *refs, spread, start):
    *out_refs, own_ref, other_ref, sems = refs
    count, wide = own_ref.shape
    copies = [
        pltpu.make_async_copy(head_hbm.at[:, pl.ds(start, wide)], own_ref, sems.at[0]),
        pltpu.make_async_copy(near_hbm, other_ref.at[: count // 2, :], sems.at[1]),
        pltpu.make_async_copy(far_hbm, other_ref.at[count // 2 :, :], sems.at[2]),
    ]
    for copy in copies:
        copy.start()
    peers = asked_ref.shape[0] // 2
    hot = [hot_rows(every_other(asked_ref, i), spread, count) for i in range(2)]
    for copy in copies:
        copy.wait()
    each = 2 * peers * spread // len(out_refs)
    for i, table in enumerate((own_ref, other_ref)):
        picked = jnp.dot(hot[i], table[...], preferred_element_type=F32).astype(BF16)
        for peer in range(peers):
            first = (2 * peer + i) * spread
            out_refs[first // each][first % each : first % each + spread, :] = picked[
                peer * spread : (peer + 1) * spread
            ]


def swapped(value, flags):
    size = value.shape[0]
    for bit, flag in enumerate(flags):
        if flag is None:
            continue
        step = 1 << bit
        other = [value[start ^ step : (start ^ step) + step] for start in range(0, size, step)]
        value = jnp.where(flag, jnp.concatenate(other, axis=0), value)
    return value


def to_pairs(value, flags):
    half = value.shape[0] // 2
    value = swapped(value, flags)
    lines = [value[j * half + i : j * half + i + 1] for i in range(half) for j in range(2)]
    return jnp.concatenate(lines, axis=0)


def from_pairs(value, flags):
    size = value.shape[0]
    lines = [value[i : i + 1] for j in range(2) for i in range(j, size, 2)]
    return swapped(jnp.concatenate(lines, axis=0), flags)


def flags_of(pack_ref, shards, used):
    lines = pack_ref[2 * shards : 2 * shards + 8, :]
    return [lines[b : b + 1] > 0.5 if use else None for b, use in enumerate(used)]


def chunks_of(refs, parts, start):
    for i in range(0, len(refs), parts):
        yield refs[i : i + parts], start
        start += refs[i].shape[1]


def score_kernel(pack_ref, mixed_hbm, late_ref, *refs, used, parts):
    *early_refs, out_ref, late_mask_ref, early_mask_ref, mixed_ref, sems = refs
    arrivals = fetch(mixed_hbm, mixed_ref, sems)
    shards, rows = out_ref.shape
    spread = late_ref.shape[0] // shards
    late = late_ref.shape[1]
    late_mask = slot_mask(pack_ref[:shards, :], spread).astype(F32)
    early_mask = slot_mask(pack_ref[shards : 2 * shards, :], spread).astype(F32)
    late_mask_ref[...] = late_mask.reshape(late_mask_ref.shape).astype(BF16)
    early_mask_ref[...] = early_mask.reshape(early_mask_ref.shape).astype(BF16)
    flags = flags_of(pack_ref, shards, used)
    for copy in arrivals:
        copy.wait()

    def scored(rows_ref, mixed, mask):
        score = lax.dot_general(
            rows_ref[...], mixed, (((1,), (1,)), ((), ())), preferred_element_type=F32
        )
        score = (score[:, :rows] + score[:, rows:]).reshape(mask.shape)
        return jnp.sum(score * mask, axis=1)

    total = scored(late_ref, mixed_ref[:, :late], late_mask)
    for group, start in chunks_of(early_refs, parts, late):
        lines, each = [], shards // parts
        for i, early_ref in enumerate(group):
            mixed = mixed_ref[:, pl.ds(start, early_ref.shape[1])]
            lines.append(scored(early_ref, mixed, early_mask[i * each : (i + 1) * each]))
        total = total + from_pairs(jnp.concatenate(lines, axis=0), flags)
    out_ref[...] = total


def grad_kernel(
    own_ref, other_ref, pack_ref, late_mask_ref, early_mask_ref, late_ref, *refs, top, used, parts
):
    *early_refs, hidden_hbm, out_ref, hidden_ref, grad_ref, sems = refs
    arrivals = fetch(hidden_hbm, hidden_ref, sems)
    layers, rows, features = hidden_ref.shape
    shards = own_ref.shape[0]
    lines = grad_ref.shape[0]
    slots = 128 * ((out_ref.shape[1] - lines) // (2 * top))
    flags = flags_of(pack_ref, shards, used)
    pack = pack_ref[2 * shards + 8 :, :]
    shard, target = pack[:top], pack[top : 2 * top]
    weight, owner, column = [pack[2 * top + i : 2 * top + i + 1] for i in range(3)]
    inverse = pack[2 * top + 3 : 2 * top + 3 + layers]
    inverse = jnp.pad(inverse, ((0, 8 - layers), (0, 0))).T

    by_shard = own_ref[...] + other_ref[...]
    number = iota((shards, rows), 0).astype(F32)
    logits = jnp.concatenate(
        [
            jnp.sum(jnp.where(shard[k : k + 1] == number, by_shard, 0.0), axis=0, keepdims=True)
            for k in range(top)
        ],
        axis=0,
    )
    logits = logits - jnp.max(logits, axis=0, keepdims=True)
    logp = logits - jnp.log(jnp.sum(jnp.exp(logits), axis=0, keepdims=True))
    grad = weight * (jnp.exp(logp) - target)
    by_shard = jnp.zeros((shards, rows), F32)
    for k in range(top):
        by_shard = jnp.where(shard[k : k + 1] == number, grad[k : k + 1], by_shard)

    def spread_out(mask, values):
        mask = mask.astype(F32).reshape(values.shape[0], -1, rows)
        return (mask * values[:, None, :]).reshape(-1, rows).astype(BF16)

    late = late_ref.shape[1]
    pairs = to_pairs(by_shard, flags)
    part = spread_out(early_mask_ref[...], pairs)
    each = part.shape[0] // parts
    part = [part[i * each : (i + 1) * each] for i in range(parts)]
    sources = [([late_ref], [spread_out(late_mask_ref[...], by_shard)], 0)]
    for group, start in chunks_of(early_refs, parts, late):
        sources.append((group, part, start))
    for copy in arrivals:
        copy.wait()
    for rows_refs, grads, start in sources:
        for cut in pieces(rows_refs[0].shape[1]):
            carried = sum(
                lax.dot_general(
                    grad, rows_ref[:, cut], (((0,), (0,)), ((), ())), preferred_element_type=F32
                )
                for rows_ref, grad in zip(rows_refs, grads)
            )
            wide, first = carried.shape[1], start + cut.start
            for layer in range(layers):
                scaled = hidden_ref[layer, :, pl.ds(first, wide)].astype(F32)
                scaled = scaled * inverse[:, layer : layer + 1]
                total = jnp.sum(scaled * carried, axis=0, keepdims=True)
                for j in range(wide // 128):
                    line = (layer * features + first) // 128 + j
                    grad_ref[line : line + 1, :] = total[:, j * 128 : (j + 1) * 128]

    high = logp.astype(BF16).astype(F32)
    halves = jnp.concatenate([high, logp - high], axis=0)
    owned = jnp.where(owner == iota((shards, 1, rows), 0).astype(F32), halves[None], 0.0)
    owned = owned.reshape(shards * 2 * top, rows).astype(BF16)
    placed = (iota((slots, rows), 0).astype(F32) == column).astype(BF16)
    sent = lax.dot_general(owned, placed, (((1,), (1,)), ((), ())), preferred_element_type=F32)
    sent = [
        sent[:, j * 128 : (j + 1) * 128].reshape(shards, 2 * top, 128) for j in range(slots // 128)
    ]
    out_ref[:, lines:, :] = jnp.concatenate(sent, axis=1).astype(BF16)
    grad = grad_ref[...].astype(BF16)
    for peer in range(shards):
        out_ref[peer, 0:lines, :] = grad


def sum_kernel(parts_ref, grad_ref, logp_ref):
    total = parts_ref[0].astype(F32)
    for peer in range(1, parts_ref.shape[0]):
        total = total + parts_ref[peer].astype(F32)
    layers, features = grad_ref.shape
    top, slots = logp_ref.shape
    each = features // 128
    for layer in range(layers):
        for j in range(each):
            line = layer * each + j
            grad_ref[layer : layer + 1, j * 128 : (j + 1) * 128] = total[line : line + 1]
    for j in range(slots // 128):
        first = layers * each + j * 2 * top
        logp_ref[:, j * 128 : (j + 1) * 128] = (
            total[first : first + top] + total[first + top : first + 2 * top]
        )


VMEM = pl.BlockSpec(memory_space=pltpu.VMEM)
HBM = pl.BlockSpec(memory_space=pltpu.HBM)


def params():
    return pltpu.CompilerParams(vmem_limit_bytes=VMEM_LIMIT)


def in_hbm(value):
    return pltpu.with_memory_space_constraint(value, pltpu.HBM)


def pick(asked, head, spread, late):
    rows = head.shape[0]
    slots, count = asked.shape[0] // 2 * spread, len(pieces(late))
    return pl.pallas_call(
        functools.partial(pick_kernel, spread=spread),
        in_specs=[VMEM, HBM],
        out_specs=HBM,
        out_shape=pltpu.HBM((slots, late), BF16),
        scratch_shapes=[
            pltpu.VMEM((rows, late), BF16),
            pltpu.VMEM((slots, late), BF16),
            pltpu.SemaphoreType.DMA((count,)),
            pltpu.SemaphoreType.DMA((count,)),
        ],
        compiler_params=params(),
        name="pick",
    )(asked, in_hbm(head))


def pick_early(asked, head, near, far, spread, start, count):
    rows, wide = head.shape[0], near.shape[1]
    slots = asked.shape[0] * spread
    return pl.pallas_call(
        functools.partial(early_kernel, spread=spread, start=start),
        in_specs=[VMEM, HBM, HBM, HBM],
        out_specs=[VMEM] * count,
        out_shape=[jax.ShapeDtypeStruct((slots // count, wide), BF16)] * count,
        scratch_shapes=[
            pltpu.VMEM((rows, wide), BF16),
            pltpu.VMEM((rows, wide), BF16),
            pltpu.SemaphoreType.DMA((3,)),
        ],
        compiler_params=params(),
        name="pick_early",
    )(asked, in_hbm(head), in_hbm(near), in_hbm(far))


def score(pack, mixed, late, early, shards, used, parts):
    rows = pack.shape[1]
    slots = sum(array.shape[0] for array in early[:parts])
    return pl.pallas_call(
        functools.partial(score_kernel, used=used, parts=parts),
        in_specs=[VMEM, HBM, VMEM] + [VMEM] * len(early),
        out_specs=[VMEM] * 3,
        out_shape=[
            jax.ShapeDtypeStruct((shards, rows), F32),
            jax.ShapeDtypeStruct((late.shape[0], rows), BF16),
            jax.ShapeDtypeStruct((slots, rows), BF16),
        ],
        scratch_shapes=[
            pltpu.VMEM(mixed.shape, BF16),
            pltpu.SemaphoreType.DMA((len(pieces(mixed.shape[1])),)),
        ],
        compiler_params=params(),
        name="score",
    )(pack, in_hbm(mixed), late, *early)


def gradient(own, other, pack, masks, late, early, hidden, lines, total_lines, top, used, parts):
    count = len(pieces(hidden.shape[2]))
    return pl.pallas_call(
        functools.partial(grad_kernel, top=top, used=used, parts=parts),
        in_specs=[VMEM] * (6 + len(early)) + [HBM],
        out_specs=VMEM,
        out_shape=jax.ShapeDtypeStruct((own.shape[0], total_lines, 128), BF16),
        scratch_shapes=[
            pltpu.VMEM(hidden.shape, BF16),
            pltpu.VMEM((lines, 128), F32),
            pltpu.SemaphoreType.DMA((count,)),
        ],
        compiler_params=params(),
        name="gradient",
    )(own, other, pack, *masks, late, *early, in_hbm(hidden))


def after(value, first):
    return lax.optimization_barrier((value, first))[0]


def add_up(parts, layers, features, top, slots):
    return pl.pallas_call(
        sum_kernel,
        in_specs=[VMEM],
        out_specs=[VMEM] * 2,
        out_shape=[
            jax.ShapeDtypeStruct((layers, features), F32),
            jax.ShapeDtypeStruct((top, slots), F32),
        ],
        compiler_params=params(),
        name="add_up",
    )(parts)


def rounded(value):
    return lax.reduce_precision(value, exponent_bits=8, mantissa_bits=7)


def position_weights(lengths, positions, sequences):
    seq_ends = jnp.cumsum(lengths)
    seq_starts = seq_ends - lengths
    position = jnp.arange(positions, dtype=jnp.int32)[None, :]
    member = (position >= seq_starts[:, None]) & (position < seq_ends[:, None])
    own_length = jnp.sum(jnp.where(member, lengths[:, None], 0), axis=0, keepdims=True)
    closing = jnp.any(member & (position == seq_ends[:, None] - 1), axis=0, keepdims=True)
    portion = 1.0 / (own_length.astype(F32) * sequences)
    return rounded(jnp.where(closing, 0.0, portion))


def swap_cores(value):
    size = lax.axis_size("mp")
    if size == 1:
        return jnp.zeros_like(value)
    return lax.ppermute(value, "mp", [(i, i ^ 1) for i in range(size)])


def exchange(value, groups=None):
    return lax.all_to_all(
        value, "dp", split_axis=0, concat_axis=0, tiled=True, axis_index_groups=groups
    )


def local(
    hidden,
    row_owner,
    candidate_shard,
    candidate_offset,
    target_logits,
    lengths,
    layer_mix,
    draft_head,
):
    rows, layers, features = hidden.shape
    top = candidate_shard.shape[1]
    peers = lax.axis_size("dp")
    cores = lax.axis_size("mp")
    capacity = max(2, 2 * rows // peers)
    spread = min(rows, max(2, 3 * rows * top // (2 * peers)))
    spread = -(-spread // 16) * 16
    half = peers // 2
    late = features - sum(CHUNKS) * features // 2048
    place, group = lax.axis_index("dp"), lax.axis_index("groups")

    count = draft_head.shape[0]
    part = count // 2
    chunks, start = [], late
    for wide in CHUNKS:
        wide = wide * features // 2048
        near = lax.dynamic_slice(draft_head, (group * part, start), (part, wide))
        near = lax.ppermute(near, "dp", [(i, (i + half) % peers) for i in range(peers)])
        chunks.append((start, near))
        start += wide

    shard = candidate_shard.T
    offset = candidate_offset.T
    number = jnp.arange(peers, dtype=jnp.int32)[:, None]
    asked = jnp.max(
        jnp.where(shard[:, None, :] == number[None], offset[:, None, :], -1), axis=0
    )
    partner = jnp.concatenate([asked[half:], asked[:half]], axis=0)
    partner = jnp.where(partner >= 0, (partner + group * part) % count, -1)
    wanted = exchange(jnp.stack([asked, partner], axis=1)).reshape(2 * peers, rows)

    picked = pick(wanted, draft_head, spread, late)
    rows_late = exchange(picked.reshape(peers, spread, late)).reshape(peers * spread, late)

    few = half <= 4
    parts = half if few else 1
    bits = [b for b in range(peers.bit_length() - 1) if few or 1 << b == half]
    used = [b in bits for b in range(peers.bit_length() - 1)]
    flags = [(place >> b) & 1 if use else None for b, use in enumerate(used)]
    wanted = lax.dynamic_slice(wanted, (place // half * half * 2, 0), (half * 2, rows))
    wanted = swapped(wanted, [None] + [None if flag is None else flag > 0 for flag in flags[:-1]])
    rows_early = []
    for start, near in chunks:
        near = after(near, picked)
        far = lax.ppermute(near, "groups", [(0, 1), (1, 0)])
        rows_here = list(pick_early(wanted, draft_head, near, far, spread, start, parts))
        if few:
            for i in range(1, half):
                rows_here[i] = lax.ppermute(rows_here[i], "dp", [(j, j ^ i) for j in range(peers)])
        else:
            halves = [list(range(half)), list(range(half, peers))]
            rows_here = exchange(rows_here[0].reshape(half, 2 * spread, -1), halves)
            rows_here = [rows_here.reshape(peers * spread, -1)]
        rows_early += rows_here

    hidden, row_owner, shard, target_logits, lengths, layer_mix = after(
        (hidden, row_owner, shard, target_logits, lengths, layer_mix), picked
    )
    tokens = hidden.transpose(1, 0, 2)
    wide = tokens.astype(F32)
    squares = jnp.sum(wide * wide, axis=2)
    squares = squares + swap_cores(squares)
    inverse = lax.rsqrt(squares / (features * cores) + EPS)
    mixed = jnp.sum(wide * layer_mix[:, None, :] * inverse[:, :, None], axis=0)
    high = rounded(mixed)
    mixed = jnp.concatenate([high, mixed - high], axis=0).astype(BF16)

    weight = position_weights(lengths[0], rows, float(lengths.shape[1] * peers))
    target = jax.nn.softmax(target_logits.T.astype(F32), axis=0)
    owner = row_owner.T
    same = (owner.T == owner) & (iota((rows, rows), 1) < iota((rows, rows), 0))
    column = lax.axis_index("dp") * capacity + jnp.sum(same.astype(jnp.int32), axis=1)[None, :]
    held = [jnp.full((1, rows), 0 if flag is None else flag, jnp.int32) for flag in flags]
    held = jnp.pad(jnp.concatenate(held, axis=0), ((0, 8 - len(held)), (0, 0)))
    pairs = to_pairs(asked, [None if flag is None else flag > 0 for flag in flags])
    pack = [asked, pairs, held, shard, target, weight, owner, column, inverse]
    pack = jnp.concatenate([value.astype(F32) for value in pack], axis=0)
    pack = jnp.pad(pack, ((0, -pack.shape[0] % 8), (0, 0)))

    slots = peers * capacity
    lines = layers * features // 128
    total_lines = lines + 2 * top * slots // 128
    own, *masks = score(pack, mixed, rows_late, rows_early, peers, used, parts)
    other = swap_cores(own)
    sent = gradient(
        own, other, pack, masks, rows_late, rows_early, tokens, lines, total_lines, top, used, parts
    )
    grad, logp = add_up(exchange(sent), layers, features, top, slots)
    return (logp.T[None], grad)


def solution(mesh):
    return jax.shard_map(
        local,
        mesh=mesh,
        in_specs=(
            P(("groups", "dp"), None, "mp"),
            P(("groups", "dp"), None),
            P(("groups", "dp"), None),
            P(("groups", "dp"), None),
            P(("groups", "dp"), None),
            P(("groups", "dp"), None),
            P(None, "mp"),
            P("dp", "mp"),
        ),
        out_specs=(P(("groups", "dp"), None, None), P("groups", "mp")),
        check_vma=False,
    )
```

```python
import functools

import jax
import jax.numpy as jnp
from jax import lax
from jax.experimental import pallas as pl
from jax.experimental.pallas import tpu as pltpu
from jax.sharding import PartitionSpec as P

EPS = 1e-06
HIGHEST = lax.Precision.HIGHEST
F32 = jnp.float32
BF16 = jnp.bfloat16
VMEM_LIMIT = 16 * 1024 * 1024
CHUNKS = (384, 256)


def iota(shape, axis):
    return lax.broadcasted_iota(jnp.int32, shape, axis)


def slot_mask(asked, spread):
    shards, rows = asked.shape
    held = asked >= 0
    earlier = (iota((rows, rows), 0) < iota((rows, rows), 1)).astype(BF16)
    rank = jnp.dot(held.astype(BF16), earlier, preferred_element_type=F32)
    rank = jnp.where(held, rank, -1.0)
    place = iota((shards, spread, rows), 1).astype(F32)
    return rank[:, None, :] == place


def pieces(features):
    return [pl.ds(start, min(512, features - start)) for start in range(0, features, 512)]


def fetch(source, target, sems):
    lead = (slice(None),) * (len(source.shape) - 1)
    copies = [
        pltpu.make_async_copy(source.at[(*lead, cut)], target.at[(*lead, cut)], sems.at[i])
        for i, cut in enumerate(pieces(source.shape[-1]))
    ]
    for copy in copies:
        copy.start()
    return copies


def hot_rows(asked, spread, count):
    shards, rows = asked.shape
    mask = slot_mask(asked, spread)
    row = jnp.where(mask, (asked.astype(F32) + 1.0)[:, None, :], 0.0)
    row = jnp.sum(row.reshape(shards * spread, rows), axis=1, keepdims=True) - 1.0
    return jnp.where(row == iota((1, count), 1).astype(F32), 1.0, 0.0).astype(BF16)


def every_other(ref, first):
    lines = [ref[i : i + 1, :] for i in range(first, ref.shape[0], 2)]
    return jnp.concatenate(lines, axis=0)


def pick_kernel(asked_ref, head_hbm, out_hbm, head_ref, picked_ref, in_sems, out_sems, *, spread):
    late = head_ref.shape[1]
    arrivals = fetch(head_hbm.at[:, :late], head_ref, in_sems)
    hot = hot_rows(every_other(asked_ref, 0), spread, head_ref.shape[0])
    departures = []
    for i, cut in enumerate(pieces(late)):
        arrivals[i].wait()
        picked_ref[:, cut] = jnp.dot(
            hot, head_ref[:, cut], preferred_element_type=F32
        ).astype(BF16)
        copy = pltpu.make_async_copy(picked_ref.at[:, cut], out_hbm.at[:, cut], out_sems.at[i])
        copy.start()
        departures.append(copy)
    for copy in departures:
        copy.wait()


def early_kernel(asked_ref, head_hbm, near_hbm, far_hbm, *refs, spread, start):
    *out_refs, own_ref, other_ref, sems = refs
    count, wide = own_ref.shape
    copies = [
        pltpu.make_async_copy(head_hbm.at[:, pl.ds(start, wide)], own_ref, sems.at[0]),
        pltpu.make_async_copy(near_hbm, other_ref.at[: count // 2, :], sems.at[1]),
        pltpu.make_async_copy(far_hbm, other_ref.at[count // 2 :, :], sems.at[2]),
    ]
    for copy in copies:
        copy.start()
    peers = asked_ref.shape[0] // 2
    hot = [hot_rows(every_other(asked_ref, i), spread, count) for i in range(2)]
    for copy in copies:
        copy.wait()
    each = 2 * peers * spread // len(out_refs)
    for i, table in enumerate((own_ref, other_ref)):
        picked = jnp.dot(hot[i], table[...], preferred_element_type=F32).astype(BF16)
        for peer in range(peers):
            first = (2 * peer + i) * spread
            out_refs[first // each][first % each : first % each + spread, :] = picked[
                peer * spread : (peer + 1) * spread
            ]


def swapped(value, flags):
    size = value.shape[0]
    for bit, flag in enumerate(flags):
        if flag is None:
            continue
        step = 1 << bit
        other = [value[start ^ step : (start ^ step) + step] for start in range(0, size, step)]
        value = jnp.where(flag, jnp.concatenate(other, axis=0), value)
    return value


def to_pairs(value, flags):
    half = value.shape[0] // 2
    value = swapped(value, flags)
    lines = [value[j * half + i : j * half + i + 1] for i in range(half) for j in range(2)]
    return jnp.concatenate(lines, axis=0)


def from_pairs(value, flags):
    size = value.shape[0]
    lines = [value[i : i + 1] for j in range(2) for i in range(j, size, 2)]
    return swapped(jnp.concatenate(lines, axis=0), flags)


def flags_of(pack_ref, shards, used):
    lines = pack_ref[2 * shards : 2 * shards + 8, :]
    return [lines[b : b + 1] > 0.5 if use else None for b, use in enumerate(used)]


def chunks_of(refs, parts, start):
    for i in range(0, len(refs), parts):
        yield refs[i : i + parts], start
        start += refs[i].shape[1]


def score_kernel(pack_ref, mixed_hbm, late_ref, *refs, used, parts):
    *early_refs, out_ref, late_mask_ref, early_mask_ref, mixed_ref, sems = refs
    arrivals = fetch(mixed_hbm, mixed_ref, sems)
    shards, rows = out_ref.shape
    spread = late_ref.shape[0] // shards
    late = late_ref.shape[1]
    late_mask = slot_mask(pack_ref[:shards, :], spread).astype(F32)
    early_mask = slot_mask(pack_ref[shards : 2 * shards, :], spread).astype(F32)
    late_mask_ref[...] = late_mask.reshape(late_mask_ref.shape).astype(BF16)
    early_mask_ref[...] = early_mask.reshape(early_mask_ref.shape).astype(BF16)
    flags = flags_of(pack_ref, shards, used)
    for copy in arrivals:
        copy.wait()

    def scored(rows_ref, mixed, mask):
        score = lax.dot_general(
            rows_ref[...], mixed, (((1,), (1,)), ((), ())), preferred_element_type=F32
        )
        score = (score[:, :rows] + score[:, rows:]).reshape(mask.shape)
        return jnp.sum(score * mask, axis=1)

    total = scored(late_ref, mixed_ref[:, :late], late_mask)
    for group, start in chunks_of(early_refs, parts, late):
        lines, each = [], shards // parts
        for i, early_ref in enumerate(group):
            mixed = mixed_ref[:, pl.ds(start, early_ref.shape[1])]
            lines.append(scored(early_ref, mixed, early_mask[i * each : (i + 1) * each]))
        total = total + from_pairs(jnp.concatenate(lines, axis=0), flags)
    out_ref[...] = total


def grad_kernel(
    own_ref, other_ref, pack_ref, late_mask_ref, early_mask_ref, late_ref, *refs, top, used, parts
):
    *early_refs, hidden_ref, out_ref, grad_ref = refs
    layers, rows, features = hidden_ref.shape
    shards = own_ref.shape[0]
    lines = grad_ref.shape[0]
    slots = 128 * ((out_ref.shape[1] - lines) // (2 * top))
    flags = flags_of(pack_ref, shards, used)
    pack = pack_ref[2 * shards + 8 :, :]
    shard, target = pack[:top], pack[top : 2 * top]
    weight, owner, column = [pack[2 * top + i : 2 * top + i + 1] for i in range(3)]
    inverse = pack[2 * top + 3 : 2 * top + 3 + layers]
    inverse = jnp.pad(inverse, ((0, 8 - layers), (0, 0))).T

    by_shard = own_ref[...] + other_ref[...]
    number = iota((shards, rows), 0).astype(F32)
    logits = jnp.concatenate(
        [
            jnp.sum(jnp.where(shard[k : k + 1] == number, by_shard, 0.0), axis=0, keepdims=True)
            for k in range(top)
        ],
        axis=0,
    )
    logits = logits - jnp.max(logits, axis=0, keepdims=True)
    logp = logits - jnp.log(jnp.sum(jnp.exp(logits), axis=0, keepdims=True))
    grad = weight * (jnp.exp(logp) - target)
    by_shard = jnp.zeros((shards, rows), F32)
    for k in range(top):
        by_shard = jnp.where(shard[k : k + 1] == number, grad[k : k + 1], by_shard)

    def spread_out(mask, values):
        mask = mask.astype(F32).reshape(values.shape[0], -1, rows)
        return (mask * values[:, None, :]).reshape(-1, rows).astype(BF16)

    late = late_ref.shape[1]
    pairs = to_pairs(by_shard, flags)
    part = spread_out(early_mask_ref[...], pairs)
    each = part.shape[0] // parts
    part = [part[i * each : (i + 1) * each] for i in range(parts)]
    sources = [([late_ref], [spread_out(late_mask_ref[...], by_shard)], 0)]
    for group, start in chunks_of(early_refs, parts, late):
        sources.append((group, part, start))
    for rows_refs, grads, start in sources:
        for cut in pieces(rows_refs[0].shape[1]):
            carried = sum(
                lax.dot_general(
                    grad, rows_ref[:, cut], (((0,), (0,)), ((), ())), preferred_element_type=F32
                )
                for rows_ref, grad in zip(rows_refs, grads)
            )
            wide, first = carried.shape[1], start + cut.start
            for layer in range(layers):
                scaled = hidden_ref[layer, :, pl.ds(first, wide)].astype(F32)
                scaled = scaled * inverse[:, layer : layer + 1]
                total = jnp.sum(scaled * carried, axis=0, keepdims=True)
                for j in range(wide // 128):
                    line = (layer * features + first) // 128 + j
                    grad_ref[line : line + 1, :] = total[:, j * 128 : (j + 1) * 128]

    high = logp.astype(BF16).astype(F32)
    halves = jnp.concatenate([high, logp - high], axis=0)
    owned = jnp.where(owner == iota((shards, 1, rows), 0).astype(F32), halves[None], 0.0)
    owned = owned.reshape(shards * 2 * top, rows).astype(BF16)
    placed = (iota((slots, rows), 0).astype(F32) == column).astype(BF16)
    sent = lax.dot_general(owned, placed, (((1,), (1,)), ((), ())), preferred_element_type=F32)
    sent = [
        sent[:, j * 128 : (j + 1) * 128].reshape(shards, 2 * top, 128) for j in range(slots // 128)
    ]
    out_ref[:, lines:, :] = jnp.concatenate(sent, axis=1).astype(BF16)
    grad = grad_ref[...].astype(BF16)
    for peer in range(shards):
        out_ref[peer, 0:lines, :] = grad


def sum_kernel(parts_ref, grad_ref, logp_ref):
    total = parts_ref[0].astype(F32)
    for peer in range(1, parts_ref.shape[0]):
        total = total + parts_ref[peer].astype(F32)
    layers, features = grad_ref.shape
    top, slots = logp_ref.shape
    each = features // 128
    for layer in range(layers):
        for j in range(each):
            line = layer * each + j
            grad_ref[layer : layer + 1, j * 128 : (j + 1) * 128] = total[line : line + 1]
    for j in range(slots // 128):
        first = layers * each + j * 2 * top
        logp_ref[:, j * 128 : (j + 1) * 128] = (
            total[first : first + top] + total[first + top : first + 2 * top]
        )


VMEM = pl.BlockSpec(memory_space=pltpu.VMEM)
HBM = pl.BlockSpec(memory_space=pltpu.HBM)


def params():
    return pltpu.CompilerParams(vmem_limit_bytes=VMEM_LIMIT)


def in_hbm(value):
    return pltpu.with_memory_space_constraint(value, pltpu.HBM)


def pick(asked, head, spread, late):
    rows = head.shape[0]
    slots, count = asked.shape[0] // 2 * spread, len(pieces(late))
    return pl.pallas_call(
        functools.partial(pick_kernel, spread=spread),
        in_specs=[VMEM, HBM],
        out_specs=HBM,
        out_shape=pltpu.HBM((slots, late), BF16),
        scratch_shapes=[
            pltpu.VMEM((rows, late), BF16),
            pltpu.VMEM((slots, late), BF16),
            pltpu.SemaphoreType.DMA((count,)),
            pltpu.SemaphoreType.DMA((count,)),
        ],
        compiler_params=params(),
        name="pick",
    )(asked, in_hbm(head))


def pick_early(asked, head, near, far, spread, start, count):
    rows, wide = head.shape[0], near.shape[1]
    slots = asked.shape[0] * spread
    return pl.pallas_call(
        functools.partial(early_kernel, spread=spread, start=start),
        in_specs=[VMEM, HBM, HBM, HBM],
        out_specs=[VMEM] * count,
        out_shape=[jax.ShapeDtypeStruct((slots // count, wide), BF16)] * count,
        scratch_shapes=[
            pltpu.VMEM((rows, wide), BF16),
            pltpu.VMEM((rows, wide), BF16),
            pltpu.SemaphoreType.DMA((3,)),
        ],
        compiler_params=params(),
        name="pick_early",
    )(asked, in_hbm(head), in_hbm(near), in_hbm(far))


def score(pack, mixed, late, early, shards, used, parts):
    rows = pack.shape[1]
    slots = sum(array.shape[0] for array in early[:parts])
    return pl.pallas_call(
        functools.partial(score_kernel, used=used, parts=parts),
        in_specs=[VMEM, HBM, VMEM] + [VMEM] * len(early),
        out_specs=[VMEM] * 3,
        out_shape=[
            jax.ShapeDtypeStruct((shards, rows), F32),
            jax.ShapeDtypeStruct((late.shape[0], rows), BF16),
            jax.ShapeDtypeStruct((slots, rows), BF16),
        ],
        scratch_shapes=[
            pltpu.VMEM(mixed.shape, BF16),
            pltpu.SemaphoreType.DMA((len(pieces(mixed.shape[1])),)),
        ],
        compiler_params=params(),
        name="score",
    )(pack, in_hbm(mixed), late, *early)


def gradient(own, other, pack, masks, late, early, hidden, lines, total_lines, top, used, parts):
    return pl.pallas_call(
        functools.partial(grad_kernel, top=top, used=used, parts=parts),
        in_specs=[VMEM] * (7 + len(early)),
        out_specs=VMEM,
        out_shape=jax.ShapeDtypeStruct((own.shape[0], total_lines, 128), BF16),
        scratch_shapes=[
            pltpu.VMEM((lines, 128), F32),
        ],
        compiler_params=params(),
        name="gradient",
    )(own, other, pack, *masks, late, *early, hidden)


def after(value, first):
    return lax.optimization_barrier((value, first))[0]


def add_up(parts, layers, features, top, slots):
    return pl.pallas_call(
        sum_kernel,
        in_specs=[VMEM],
        out_specs=[VMEM] * 2,
        out_shape=[
            jax.ShapeDtypeStruct((layers, features), F32),
            jax.ShapeDtypeStruct((top, slots), F32),
        ],
        compiler_params=params(),
        name="add_up",
    )(parts)


def rounded(value):
    return lax.reduce_precision(value, exponent_bits=8, mantissa_bits=7)


def position_weights(lengths, positions, sequences):
    seq_ends = jnp.cumsum(lengths)
    seq_starts = seq_ends - lengths
    position = jnp.arange(positions, dtype=jnp.int32)[None, :]
    member = (position >= seq_starts[:, None]) & (position < seq_ends[:, None])
    own_length = jnp.sum(jnp.where(member, lengths[:, None], 0), axis=0, keepdims=True)
    closing = jnp.any(member & (position == seq_ends[:, None] - 1), axis=0, keepdims=True)
    portion = 1.0 / (own_length.astype(F32) * sequences)
    return rounded(jnp.where(closing, 0.0, portion))


def swap_cores(value):
    size = lax.axis_size("mp")
    if size == 1:
        return jnp.zeros_like(value)
    return lax.ppermute(value, "mp", [(i, i ^ 1) for i in range(size)])


def exchange(value, groups=None):
    return lax.all_to_all(
        value, "dp", split_axis=0, concat_axis=0, tiled=True, axis_index_groups=groups
    )


def local(
    hidden,
    row_owner,
    candidate_shard,
    candidate_offset,
    target_logits,
    lengths,
    layer_mix,
    draft_head,
):
    rows, layers, features = hidden.shape
    top = candidate_shard.shape[1]
    peers = lax.axis_size("dp")
    cores = lax.axis_size("mp")
    capacity = max(2, 2 * rows // peers)
    spread = min(rows, max(2, 3 * rows * top // (2 * peers)))
    spread = -(-spread // 16) * 16
    half = peers // 2
    late = features - sum(CHUNKS) * features // 2048
    place, group = lax.axis_index("dp"), lax.axis_index("groups")

    count = draft_head.shape[0]
    part = count // 2
    chunks, start = [], late
    for wide in CHUNKS:
        wide = wide * features // 2048
        near = lax.dynamic_slice(draft_head, (group * part, start), (part, wide))
        near = lax.ppermute(near, "dp", [(i, (i + half) % peers) for i in range(peers)])
        chunks.append((start, near))
        start += wide

    shard = candidate_shard.T
    offset = candidate_offset.T
    line = jnp.arange(2 * peers, dtype=jnp.int32)[:, None]
    number = (line // 2 + line % 2 * half) % peers
    placed = (offset[:, None, :] + line[None] % 2 * (group * part)) % count
    message = jnp.max(jnp.where(shard[:, None, :] == number[None], placed, -1), axis=0)
    wanted = exchange(message.reshape(peers, 2, rows)).reshape(2 * peers, rows)

    picked = pick(wanted, draft_head, spread, late)
    rows_late = exchange(picked.reshape(peers, spread, late)).reshape(peers * spread, late)

    few = half <= 4
    parts = half if few else 1
    bits = [b for b in range(peers.bit_length() - 1) if few or 1 << b == half]
    used = [b in bits for b in range(peers.bit_length() - 1)]
    flags = [(place >> b) & 1 if use else None for b, use in enumerate(used)]
    wanted = lax.dynamic_slice(wanted, (place // half * half * 2, 0), (half * 2, rows))
    wanted = swapped(wanted, [None] + [None if flag is None else flag > 0 for flag in flags[:-1]])
    rows_early = []
    for start, near in chunks:
        near = after(near, picked)
        far = lax.ppermute(near, "groups", [(0, 1), (1, 0)])
        rows_here = list(pick_early(wanted, draft_head, near, far, spread, start, parts))
        if few:
            for i in range(1, half):
                rows_here[i] = lax.ppermute(rows_here[i], "dp", [(j, j ^ i) for j in range(peers)])
        else:
            halves = [list(range(half)), list(range(half, peers))]
            rows_here = exchange(rows_here[0].reshape(half, 2 * spread, -1), halves)
            rows_here = [rows_here.reshape(peers * spread, -1)]
        rows_early += rows_here

    hidden, layer_mix = after((hidden, layer_mix), picked)
    number = jnp.arange(peers, dtype=jnp.int32)[:, None]
    asked = jnp.max(
        jnp.where(shard[:, None, :] == number[None], offset[:, None, :], -1), axis=0
    )
    tokens = hidden.transpose(1, 0, 2)
    wide = tokens.astype(F32)
    squares = jnp.sum(wide * wide, axis=2)
    squares = squares + swap_cores(squares)
    inverse = lax.rsqrt(squares / (features * cores) + EPS)
    mixed = jnp.sum(wide * layer_mix[:, None, :] * inverse[:, :, None], axis=0)
    high = rounded(mixed)
    mixed = jnp.concatenate([high, mixed - high], axis=0).astype(BF16)

    weight = position_weights(lengths[0], rows, float(lengths.shape[1] * peers))
    target = jax.nn.softmax(target_logits.T.astype(F32), axis=0)
    owner = row_owner.T
    same = (owner.T == owner) & (iota((rows, rows), 1) < iota((rows, rows), 0))
    column = lax.axis_index("dp") * capacity + jnp.sum(same.astype(jnp.int32), axis=1)[None, :]
    held = [jnp.full((1, rows), 0 if flag is None else flag, jnp.int32) for flag in flags]
    held = jnp.pad(jnp.concatenate(held, axis=0), ((0, 8 - len(held)), (0, 0)))
    pairs = to_pairs(asked, [None if flag is None else flag > 0 for flag in flags])
    pack = [asked, pairs, held, shard, target, weight, owner, column, inverse]
    pack = jnp.concatenate([value.astype(F32) for value in pack], axis=0)
    pack = jnp.pad(pack, ((0, -pack.shape[0] % 8), (0, 0)))

    slots = peers * capacity
    lines = layers * features // 128
    total_lines = lines + 2 * top * slots // 128
    own, *masks = score(pack, mixed, rows_late, rows_early, peers, used, parts)
    other = swap_cores(own)
    sent = gradient(
        own, other, pack, masks, rows_late, rows_early, tokens, lines, total_lines, top, used, parts
    )
    grad, logp = add_up(exchange(sent), layers, features, top, slots)
    return (logp.T[None], grad)


def solution(mesh):
    return jax.shard_map(
        local,
        mesh=mesh,
        in_specs=(
            P(("groups", "dp"), None, "mp"),
            P(("groups", "dp"), None),
            P(("groups", "dp"), None),
            P(("groups", "dp"), None),
            P(("groups", "dp"), None),
            P(("groups", "dp"), None),
            P(None, "mp"),
            P("dp", "mp"),
        ),
        out_specs=(P(("groups", "dp"), None, None), P("groups", "mp")),
        check_vma=False,
    )
```

```python
import functools

import jax
import jax.numpy as jnp
from jax import lax
from jax.experimental import pallas as pl
from jax.experimental.pallas import tpu as pltpu
from jax.sharding import PartitionSpec as P

EPS = 1e-06
HIGHEST = lax.Precision.HIGHEST
F32 = jnp.float32
BF16 = jnp.bfloat16
VMEM_LIMIT = 16 * 1024 * 1024
CHUNKS = (512, 128)


def iota(shape, axis):
    return lax.broadcasted_iota(jnp.int32, shape, axis)


def slot_mask(asked, spread):
    shards, rows = asked.shape
    held = asked >= 0
    earlier = (iota((rows, rows), 0) < iota((rows, rows), 1)).astype(BF16)
    rank = jnp.dot(held.astype(BF16), earlier, preferred_element_type=F32)
    rank = jnp.where(held, rank, -1.0)
    place = iota((shards, spread, rows), 1).astype(F32)
    return rank[:, None, :] == place


def pieces(features):
    return [pl.ds(start, min(512, features - start)) for start in range(0, features, 512)]


def fetch(source, target, sems):
    lead = (slice(None),) * (len(source.shape) - 1)
    copies = [
        pltpu.make_async_copy(source.at[(*lead, cut)], target.at[(*lead, cut)], sems.at[i])
        for i, cut in enumerate(pieces(source.shape[-1]))
    ]
    for copy in copies:
        copy.start()
    return copies


def hot_rows(asked, spread, count):
    shards, rows = asked.shape
    mask = slot_mask(asked, spread)
    row = jnp.where(mask, (asked.astype(F32) + 1.0)[:, None, :], 0.0)
    row = jnp.sum(row.reshape(shards * spread, rows), axis=1, keepdims=True) - 1.0
    return jnp.where(row == iota((1, count), 1).astype(F32), 1.0, 0.0).astype(BF16)


def every_other(ref, first):
    lines = [ref[i : i + 1, :] for i in range(first, ref.shape[0], 2)]
    return jnp.concatenate(lines, axis=0)


def pick_kernel(asked_ref, head_hbm, out_hbm, head_ref, picked_ref, in_sems, out_sems, *, spread):
    late = head_ref.shape[1]
    arrivals = fetch(head_hbm.at[:, :late], head_ref, in_sems)
    hot = hot_rows(every_other(asked_ref, 0), spread, head_ref.shape[0])
    departures = []
    for i, cut in enumerate(pieces(late)):
        arrivals[i].wait()
        picked_ref[:, cut] = jnp.dot(
            hot, head_ref[:, cut], preferred_element_type=F32
        ).astype(BF16)
        copy = pltpu.make_async_copy(picked_ref.at[:, cut], out_hbm.at[:, cut], out_sems.at[i])
        copy.start()
        departures.append(copy)
    for copy in departures:
        copy.wait()


def early_kernel(asked_ref, head_hbm, near_ref, far_ref, *refs, spread, start):
    *out_refs, own_ref, sent_ref, sems = refs
    count, wide = own_ref.shape
    copy = pltpu.make_async_copy(head_hbm.at[:, pl.ds(start, wide)], own_ref, sems.at[0])
    copy.start()
    peers = asked_ref.shape[0] // 2
    hot = [hot_rows(every_other(asked_ref, i), spread, count) for i in range(2)]
    other = sum(
        jnp.dot(
            hot[1][:, j * count // 2 : (j + 1) * count // 2],
            ref[...],
            preferred_element_type=F32,
        )
        for j, ref in enumerate((near_ref, far_ref))
    )
    copy.wait()
    own = jnp.dot(hot[0], own_ref[...], preferred_element_type=F32)
    each = 2 * peers * spread // len(out_refs)
    targets = [out_refs[0]] + [sent_ref.at[i] for i in range(len(out_refs) - 1)]
    for i, picked in enumerate((own.astype(BF16), other.astype(BF16))):
        for peer in range(peers):
            first = (2 * peer + i) * spread
            targets[first // each][first % each : first % each + spread, :] = picked[
                peer * spread : (peer + 1) * spread
            ]
    copies = [
        pltpu.make_async_copy(sent_ref.at[i], out_ref, sems.at[1 + i])
        for i, out_ref in enumerate(out_refs[1:])
    ]
    for copy in copies:
        copy.start()
    for copy in copies:
        copy.wait()


def swapped(value, flags):
    size = value.shape[0]
    for bit, flag in enumerate(flags):
        if flag is None:
            continue
        step = 1 << bit
        other = [value[start ^ step : (start ^ step) + step] for start in range(0, size, step)]
        value = jnp.where(flag, jnp.concatenate(other, axis=0), value)
    return value


def to_pairs(value, flags):
    half = value.shape[0] // 2
    value = swapped(value, flags)
    lines = [value[j * half + i : j * half + i + 1] for i in range(half) for j in range(2)]
    return jnp.concatenate(lines, axis=0)


def from_pairs(value, flags):
    size = value.shape[0]
    lines = [value[i : i + 1] for j in range(2) for i in range(j, size, 2)]
    return swapped(jnp.concatenate(lines, axis=0), flags)


def flags_of(pack_ref, shards, used):
    lines = pack_ref[2 * shards : 2 * shards + 8, :]
    return [lines[b : b + 1] > 0.5 if use else None for b, use in enumerate(used)]


def chunks_of(refs, parts, start):
    for i in range(0, len(refs), parts):
        yield refs[i : i + parts], start
        start += refs[i].shape[1]


def score_kernel(pack_ref, mixed_hbm, late_ref, *refs, used, parts):
    *early_refs, out_ref, late_mask_ref, early_mask_ref, mixed_ref, sems = refs
    arrivals = fetch(mixed_hbm, mixed_ref, sems)
    shards, rows = out_ref.shape
    spread = late_ref.shape[0] // shards
    late = late_ref.shape[1]
    late_mask = slot_mask(pack_ref[:shards, :], spread).astype(F32)
    early_mask = slot_mask(pack_ref[shards : 2 * shards, :], spread).astype(F32)
    late_mask_ref[...] = late_mask.reshape(late_mask_ref.shape).astype(BF16)
    early_mask_ref[...] = early_mask.reshape(early_mask_ref.shape).astype(BF16)
    flags = flags_of(pack_ref, shards, used)
    for copy in arrivals:
        copy.wait()

    def scored(rows_ref, mixed, mask):
        score = lax.dot_general(
            rows_ref[...], mixed, (((1,), (1,)), ((), ())), preferred_element_type=F32
        )
        score = (score[:, :rows] + score[:, rows:]).reshape(mask.shape)
        return jnp.sum(score * mask, axis=1)

    total = scored(late_ref, mixed_ref[:, :late], late_mask)
    for group, start in chunks_of(early_refs, parts, late):
        lines, each = [], shards // parts
        for i, early_ref in enumerate(group):
            mixed = mixed_ref[:, pl.ds(start, early_ref.shape[1])]
            lines.append(scored(early_ref, mixed, early_mask[i * each : (i + 1) * each]))
        total = total + from_pairs(jnp.concatenate(lines, axis=0), flags)
    out_ref[...] = total


def grad_kernel(
    own_ref, other_ref, pack_ref, late_mask_ref, early_mask_ref, late_ref, *refs, top, used, parts
):
    *early_refs, hidden_ref, out_ref, grad_ref = refs
    layers, rows, features = hidden_ref.shape
    shards = own_ref.shape[0]
    lines = grad_ref.shape[0]
    slots = 128 * ((out_ref.shape[1] - lines) // (2 * top))
    flags = flags_of(pack_ref, shards, used)
    pack = pack_ref[2 * shards + 8 :, :]
    shard, target = pack[:top], pack[top : 2 * top]
    weight, owner, column = [pack[2 * top + i : 2 * top + i + 1] for i in range(3)]
    inverse = pack[2 * top + 3 : 2 * top + 3 + layers]
    inverse = jnp.pad(inverse, ((0, 8 - layers), (0, 0))).T

    by_shard = own_ref[...] + other_ref[...]
    number = iota((shards, rows), 0).astype(F32)
    logits = jnp.concatenate(
        [
            jnp.sum(jnp.where(shard[k : k + 1] == number, by_shard, 0.0), axis=0, keepdims=True)
            for k in range(top)
        ],
        axis=0,
    )
    logits = logits - jnp.max(logits, axis=0, keepdims=True)
    logp = logits - jnp.log(jnp.sum(jnp.exp(logits), axis=0, keepdims=True))
    grad = weight * (jnp.exp(logp) - target)
    by_shard = jnp.zeros((shards, rows), F32)
    for k in range(top):
        by_shard = jnp.where(shard[k : k + 1] == number, grad[k : k + 1], by_shard)

    def spread_out(mask, values):
        mask = mask.astype(F32).reshape(values.shape[0], -1, rows)
        return (mask * values[:, None, :]).reshape(-1, rows).astype(BF16)

    late = late_ref.shape[1]
    pairs = to_pairs(by_shard, flags)
    part = spread_out(early_mask_ref[...], pairs)
    each = part.shape[0] // parts
    part = [part[i * each : (i + 1) * each] for i in range(parts)]
    sources = [([late_ref], [spread_out(late_mask_ref[...], by_shard)], 0)]
    for group, start in chunks_of(early_refs, parts, late):
        sources.append((group, part, start))
    for rows_refs, grads, start in sources:
        for cut in pieces(rows_refs[0].shape[1]):
            carried = sum(
                lax.dot_general(
                    grad, rows_ref[:, cut], (((0,), (0,)), ((), ())), preferred_element_type=F32
                )
                for rows_ref, grad in zip(rows_refs, grads)
            )
            wide, first = carried.shape[1], start + cut.start
            for layer in range(layers):
                scaled = hidden_ref[layer, :, pl.ds(first, wide)].astype(F32)
                scaled = scaled * inverse[:, layer : layer + 1]
                total = jnp.sum(scaled * carried, axis=0, keepdims=True)
                for j in range(wide // 128):
                    line = (layer * features + first) // 128 + j
                    grad_ref[line : line + 1, :] = total[:, j * 128 : (j + 1) * 128]

    high = logp.astype(BF16).astype(F32)
    halves = jnp.concatenate([high, logp - high], axis=0)
    owned = jnp.where(owner == iota((shards, 1, rows), 0).astype(F32), halves[None], 0.0)
    owned = owned.reshape(shards * 2 * top, rows).astype(BF16)
    placed = (iota((slots, rows), 0).astype(F32) == column).astype(BF16)
    sent = lax.dot_general(owned, placed, (((1,), (1,)), ((), ())), preferred_element_type=F32)
    sent = [
        sent[:, j * 128 : (j + 1) * 128].reshape(shards, 2 * top, 128) for j in range(slots // 128)
    ]
    out_ref[:, lines:, :] = jnp.concatenate(sent, axis=1).astype(BF16)
    grad = grad_ref[...].astype(BF16)
    for peer in range(shards):
        out_ref[peer, 0:lines, :] = grad


def sum_kernel(parts_ref, grad_ref, logp_ref):
    total = parts_ref[0].astype(F32)
    for peer in range(1, parts_ref.shape[0]):
        total = total + parts_ref[peer].astype(F32)
    layers, features = grad_ref.shape
    top, slots = logp_ref.shape
    each = features // 128
    for layer in range(layers):
        for j in range(each):
            line = layer * each + j
            grad_ref[layer : layer + 1, j * 128 : (j + 1) * 128] = total[line : line + 1]
    for j in range(slots // 128):
        first = layers * each + j * 2 * top
        logp_ref[:, j * 128 : (j + 1) * 128] = (
            total[first : first + top] + total[first + top : first + 2 * top]
        )


VMEM = pl.BlockSpec(memory_space=pltpu.VMEM)
HBM = pl.BlockSpec(memory_space=pltpu.HBM)


def params():
    return pltpu.CompilerParams(vmem_limit_bytes=VMEM_LIMIT)


def in_hbm(value):
    return pltpu.with_memory_space_constraint(value, pltpu.HBM)


def pick(asked, head, spread, late):
    rows = head.shape[0]
    slots, count = asked.shape[0] // 2 * spread, len(pieces(late))
    return pl.pallas_call(
        functools.partial(pick_kernel, spread=spread),
        in_specs=[VMEM, HBM],
        out_specs=HBM,
        out_shape=pltpu.HBM((slots, late), BF16),
        scratch_shapes=[
            pltpu.VMEM((rows, late), BF16),
            pltpu.VMEM((slots, late), BF16),
            pltpu.SemaphoreType.DMA((count,)),
            pltpu.SemaphoreType.DMA((count,)),
        ],
        compiler_params=params(),
        name="pick",
    )(asked, in_hbm(head))


def pick_early(asked, head, near, far, spread, start, count):
    rows, wide = head.shape[0], near.shape[1]
    slots = asked.shape[0] * spread
    return pl.pallas_call(
        functools.partial(early_kernel, spread=spread, start=start),
        in_specs=[VMEM, HBM, VMEM, VMEM],
        out_specs=[VMEM] + [HBM] * (count - 1),
        out_shape=[jax.ShapeDtypeStruct((slots // count, wide), BF16)]
        + [pltpu.HBM((slots // count, wide), BF16)] * (count - 1),
        scratch_shapes=[
            pltpu.VMEM((rows, wide), BF16),
            pltpu.VMEM((max(1, count - 1), slots // count, wide), BF16),
            pltpu.SemaphoreType.DMA((count,)),
        ],
        compiler_params=params(),
        name="pick_early",
    )(asked, in_hbm(head), near, far)


def score(pack, mixed, late, early, shards, used, parts):
    rows = pack.shape[1]
    slots = sum(array.shape[0] for array in early[:parts])
    return pl.pallas_call(
        functools.partial(score_kernel, used=used, parts=parts),
        in_specs=[VMEM, HBM, VMEM] + [VMEM] * len(early),
        out_specs=[VMEM] * 3,
        out_shape=[
            jax.ShapeDtypeStruct((shards, rows), F32),
            jax.ShapeDtypeStruct((late.shape[0], rows), BF16),
            jax.ShapeDtypeStruct((slots, rows), BF16),
        ],
        scratch_shapes=[
            pltpu.VMEM(mixed.shape, BF16),
            pltpu.SemaphoreType.DMA((len(pieces(mixed.shape[1])),)),
        ],
        compiler_params=params(),
        name="score",
    )(pack, in_hbm(mixed), late, *early)


def gradient(own, other, pack, masks, late, early, hidden, lines, total_lines, top, used, parts):
    return pl.pallas_call(
        functools.partial(grad_kernel, top=top, used=used, parts=parts),
        in_specs=[VMEM] * (7 + len(early)),
        out_specs=VMEM,
        out_shape=jax.ShapeDtypeStruct((own.shape[0], total_lines, 128), BF16),
        scratch_shapes=[
            pltpu.VMEM((lines, 128), F32),
        ],
        compiler_params=params(),
        name="gradient",
    )(own, other, pack, *masks, late, *early, hidden)


def after(value, first):
    return lax.optimization_barrier((value, first))[0]


def add_up(parts, layers, features, top, slots):
    return pl.pallas_call(
        sum_kernel,
        in_specs=[VMEM],
        out_specs=[VMEM] * 2,
        out_shape=[
            jax.ShapeDtypeStruct((layers, features), F32),
            jax.ShapeDtypeStruct((top, slots), F32),
        ],
        compiler_params=params(),
        name="add_up",
    )(parts)


def rounded(value):
    return lax.reduce_precision(value, exponent_bits=8, mantissa_bits=7)


def position_weights(lengths, positions, sequences):
    seq_ends = jnp.cumsum(lengths)
    seq_starts = seq_ends - lengths
    position = jnp.arange(positions, dtype=jnp.int32)[None, :]
    member = (position >= seq_starts[:, None]) & (position < seq_ends[:, None])
    own_length = jnp.sum(jnp.where(member, lengths[:, None], 0), axis=0, keepdims=True)
    closing = jnp.any(member & (position == seq_ends[:, None] - 1), axis=0, keepdims=True)
    portion = 1.0 / (own_length.astype(F32) * sequences)
    return rounded(jnp.where(closing, 0.0, portion))


def swap_cores(value):
    size = lax.axis_size("mp")
    if size == 1:
        return jnp.zeros_like(value)
    return lax.ppermute(value, "mp", [(i, i ^ 1) for i in range(size)])


def exchange(value, groups=None):
    return lax.all_to_all(
        value, "dp", split_axis=0, concat_axis=0, tiled=True, axis_index_groups=groups
    )


def local(
    hidden,
    row_owner,
    candidate_shard,
    candidate_offset,
    target_logits,
    lengths,
    layer_mix,
    draft_head,
):
    rows, layers, features = hidden.shape
    top = candidate_shard.shape[1]
    peers = lax.axis_size("dp")
    cores = lax.axis_size("mp")
    capacity = max(2, 2 * rows // peers)
    spread = min(rows, max(2, 3 * rows * top // (2 * peers)))
    spread = -(-spread // 16) * 16
    half = peers // 2
    late = features - sum(CHUNKS) * features // 2048
    place, group = lax.axis_index("dp"), lax.axis_index("groups")

    count = draft_head.shape[0]
    part = count // 2
    chunks, start = [], late
    for wide in CHUNKS:
        wide = wide * features // 2048
        near = lax.dynamic_slice(draft_head, (group * part, start), (part, wide))
        near = lax.ppermute(near, "dp", [(i, (i + half) % peers) for i in range(peers)])
        chunks.append((start, near))
        start += wide

    shard = candidate_shard.T
    offset = candidate_offset.T
    line = jnp.arange(2 * peers, dtype=jnp.int32)[:, None]
    number = (line // 2 + line % 2 * half) % peers
    placed = (offset[:, None, :] + line[None] % 2 * (group * part)) % count
    message = jnp.max(jnp.where(shard[:, None, :] == number[None], placed, -1), axis=0)
    wanted = exchange(message.reshape(peers, 2, rows)).reshape(2 * peers, rows)

    picked = pick(wanted, draft_head, spread, late)
    rows_late = exchange(picked.reshape(peers, spread, late)).reshape(peers * spread, late)

    few = half <= 4
    parts = half if few else 1
    bits = [b for b in range(peers.bit_length() - 1) if few or 1 << b == half]
    used = [b in bits for b in range(peers.bit_length() - 1)]
    flags = [(place >> b) & 1 if use else None for b, use in enumerate(used)]
    wanted = lax.dynamic_slice(wanted, (place // half * half * 2, 0), (half * 2, rows))
    wanted = swapped(wanted, [None] + [None if flag is None else flag > 0 for flag in flags[:-1]])
    rows_early = []
    for start, near in chunks:
        near = after(near, picked)
        far = lax.ppermute(near, "groups", [(0, 1), (1, 0)])
        rows_here = list(pick_early(wanted, draft_head, near, far, spread, start, parts))
        if few:
            for i in range(1, half):
                rows_here[i] = lax.ppermute(rows_here[i], "dp", [(j, j ^ i) for j in range(peers)])
        else:
            halves = [list(range(half)), list(range(half, peers))]
            rows_here = exchange(rows_here[0].reshape(half, 2 * spread, -1), halves)
            rows_here = [rows_here.reshape(peers * spread, -1)]
        rows_early += rows_here

    hidden, layer_mix = after((hidden, layer_mix), picked)
    number = jnp.arange(peers, dtype=jnp.int32)[:, None]
    asked = jnp.max(
        jnp.where(shard[:, None, :] == number[None], offset[:, None, :], -1), axis=0
    )
    tokens = hidden.transpose(1, 0, 2)
    wide = tokens.astype(F32)
    squares = jnp.sum(wide * wide, axis=2)
    squares = squares + swap_cores(squares)
    inverse = lax.rsqrt(squares / (features * cores) + EPS)
    mixed = jnp.sum(wide * layer_mix[:, None, :] * inverse[:, :, None], axis=0)
    high = rounded(mixed)
    mixed = jnp.concatenate([high, mixed - high], axis=0).astype(BF16)

    weight = position_weights(lengths[0], rows, float(lengths.shape[1] * peers))
    target = jax.nn.softmax(target_logits.T.astype(F32), axis=0)
    owner = row_owner.T
    same = (owner.T == owner) & (iota((rows, rows), 1) < iota((rows, rows), 0))
    column = lax.axis_index("dp") * capacity + jnp.sum(same.astype(jnp.int32), axis=1)[None, :]
    held = [jnp.full((1, rows), 0 if flag is None else flag, jnp.int32) for flag in flags]
    held = jnp.pad(jnp.concatenate(held, axis=0), ((0, 8 - len(held)), (0, 0)))
    pairs = to_pairs(asked, [None if flag is None else flag > 0 for flag in flags])
    pack = [asked, pairs, held, shard, target, weight, owner, column, inverse]
    pack = jnp.concatenate([value.astype(F32) for value in pack], axis=0)
    pack = jnp.pad(pack, ((0, -pack.shape[0] % 8), (0, 0)))

    slots = peers * capacity
    lines = layers * features // 128
    total_lines = lines + 2 * top * slots // 128
    own, *masks = score(pack, mixed, rows_late, rows_early, peers, used, parts)
    other = swap_cores(own)
    sent = gradient(
        own, other, pack, masks, rows_late, rows_early, tokens, lines, total_lines, top, used, parts
    )
    grad, logp = add_up(exchange(sent), layers, features, top, slots)
    return (logp.T[None], grad)


def solution(mesh):
    return jax.shard_map(
        local,
        mesh=mesh,
        in_specs=(
            P(("groups", "dp"), None, "mp"),
            P(("groups", "dp"), None),
            P(("groups", "dp"), None),
            P(("groups", "dp"), None),
            P(("groups", "dp"), None),
            P(("groups", "dp"), None),
            P(None, "mp"),
            P("dp", "mp"),
        ),
        out_specs=(P(("groups", "dp"), None, None), P("groups", "mp")),
        check_vma=False,
    )
```

```python
import functools

import jax
import jax.numpy as jnp
from jax import lax
from jax.experimental import pallas as pl
from jax.experimental.pallas import tpu as pltpu
from jax.sharding import PartitionSpec as P

EPS = 1e-06
HIGHEST = lax.Precision.HIGHEST
F32 = jnp.float32
BF16 = jnp.bfloat16
VMEM_LIMIT = 16 * 1024 * 1024
CHUNKS = (256, 384)


def iota(shape, axis):
    return lax.broadcasted_iota(jnp.int32, shape, axis)


def slot_mask(asked, spread):
    shards, rows = asked.shape
    held = asked >= 0
    earlier = (iota((rows, rows), 0) < iota((rows, rows), 1)).astype(BF16)
    rank = jnp.dot(held.astype(BF16), earlier, preferred_element_type=F32)
    rank = jnp.where(held, rank, -1.0)
    place = iota((shards, spread, rows), 1).astype(F32)
    return rank[:, None, :] == place


def pieces(features):
    return [pl.ds(start, min(512, features - start)) for start in range(0, features, 512)]


def fetch(source, target, sems):
    lead = (slice(None),) * (len(source.shape) - 1)
    copies = [
        pltpu.make_async_copy(source.at[(*lead, cut)], target.at[(*lead, cut)], sems.at[i])
        for i, cut in enumerate(pieces(source.shape[-1]))
    ]
    for copy in copies:
        copy.start()
    return copies


def hot_rows(asked, spread, count):
    shards, rows = asked.shape
    mask = slot_mask(asked, spread)
    row = jnp.where(mask, (asked.astype(F32) + 1.0)[:, None, :], 0.0)
    row = jnp.sum(row.reshape(shards * spread, rows), axis=1, keepdims=True) - 1.0
    return jnp.where(row == iota((1, count), 1).astype(F32), 1.0, 0.0).astype(BF16)


def every_other(ref, first):
    lines = [ref[i : i + 1, :] for i in range(first, ref.shape[0], 2)]
    return jnp.concatenate(lines, axis=0)


def pick_kernel(asked_ref, head_hbm, out_hbm, head_ref, picked_ref, in_sems, out_sems, *, spread):
    late = head_ref.shape[1]
    arrivals = fetch(head_hbm.at[:, :late], head_ref, in_sems)
    hot = hot_rows(every_other(asked_ref, 0), spread, head_ref.shape[0])
    departures = []
    for i, cut in enumerate(pieces(late)):
        arrivals[i].wait()
        picked_ref[:, cut] = jnp.dot(
            hot, head_ref[:, cut], preferred_element_type=F32
        ).astype(BF16)
        copy = pltpu.make_async_copy(picked_ref.at[:, cut], out_hbm.at[:, cut], out_sems.at[i])
        copy.start()
        departures.append(copy)
    for copy in departures:
        copy.wait()


def begin_kernel(
    group_ref, shard_hbm, offset_hbm, head_hbm, message_hbm, *refs, peers, starts
):
    *out_refs, shard_ref, offset_ref, message_ref, sems = refs
    small = [
        pltpu.make_async_copy(shard_hbm, shard_ref, sems.at[0]),
        pltpu.make_async_copy(offset_hbm, offset_ref, sems.at[1]),
    ]
    large = []
    part = out_refs[0].shape[0]
    shift = group_ref[0] * part
    for i, out_ref in enumerate(out_refs):
        rows = pl.ds(pl.multiple_of(shift, part), part)
        source = head_hbm.at[rows, pl.ds(starts[i], out_ref.shape[1])]
        large.append(pltpu.make_async_copy(source, out_ref, sems.at[3 + i]))
    for copy in small + large:
        copy.start()
    for copy in small:
        copy.wait()
    shard, offset = shard_ref[...], offset_ref[...]
    count = head_hbm.shape[0]
    other = offset + shift
    other = jnp.where(other >= count, other - count, other)
    line = iota(message_ref.shape, 0)
    number = line // 2 + jnp.where(line % 2 == 0, 0, peers // 2)
    number = jnp.where(number >= peers, number - peers, number)
    message = jnp.full(message_ref.shape, -1, jnp.int32)
    for k in range(shard.shape[0]):
        asked = jnp.where(line % 2 == 0, offset[k : k + 1], other[k : k + 1])
        message = jnp.where(shard[k : k + 1] == number, asked, message)
    message_ref[...] = message
    copy = pltpu.make_async_copy(message_ref, message_hbm, sems.at[2])
    copy.start()
    copy.wait()
    for copy in large:
        copy.wait()


def early_kernel(asked_ref, head_hbm, near_ref, far_ref, *refs, spread, start):
    *out_refs, own_ref, sent_ref, sems = refs
    count, wide = own_ref.shape
    copy = pltpu.make_async_copy(head_hbm.at[:, pl.ds(start, wide)], own_ref, sems.at[0])
    copy.start()
    peers = asked_ref.shape[0] // 2
    hot = [hot_rows(every_other(asked_ref, i), spread, count) for i in range(2)]
    other = sum(
        jnp.dot(
            hot[1][:, j * count // 2 : (j + 1) * count // 2],
            ref[...],
            preferred_element_type=F32,
        )
        for j, ref in enumerate((near_ref, far_ref))
    )
    copy.wait()
    own = jnp.dot(hot[0], own_ref[...], preferred_element_type=F32)
    each = 2 * peers * spread // len(out_refs)
    targets = [out_refs[0]] + [sent_ref.at[i] for i in range(len(out_refs) - 1)]
    for i, picked in enumerate((own.astype(BF16), other.astype(BF16))):
        for peer in range(peers):
            first = (2 * peer + i) * spread
            targets[first // each][first % each : first % each + spread, :] = picked[
                peer * spread : (peer + 1) * spread
            ]
    copies = [
        pltpu.make_async_copy(sent_ref.at[i], out_ref, sems.at[1 + i])
        for i, out_ref in enumerate(out_refs[1:])
    ]
    for copy in copies:
        copy.start()
    for copy in copies:
        copy.wait()


def swapped(value, flags):
    size = value.shape[0]
    for bit, flag in enumerate(flags):
        if flag is None:
            continue
        step = 1 << bit
        other = [value[start ^ step : (start ^ step) + step] for start in range(0, size, step)]
        value = jnp.where(flag, jnp.concatenate(other, axis=0), value)
    return value


def to_pairs(value, flags):
    half = value.shape[0] // 2
    value = swapped(value, flags)
    lines = [value[j * half + i : j * half + i + 1] for i in range(half) for j in range(2)]
    return jnp.concatenate(lines, axis=0)


def from_pairs(value, flags):
    size = value.shape[0]
    lines = [value[i : i + 1] for j in range(2) for i in range(j, size, 2)]
    return swapped(jnp.concatenate(lines, axis=0), flags)


def flags_of(pack_ref, shards, used):
    lines = pack_ref[2 * shards : 2 * shards + 8, :]
    return [lines[b : b + 1] > 0.5 if use else None for b, use in enumerate(used)]


def chunks_of(refs, parts, start):
    for i in range(0, len(refs), parts):
        yield refs[i : i + parts], start
        start += refs[i].shape[1]


def score_kernel(pack_ref, mixed_hbm, late_ref, *refs, used, parts):
    *early_refs, out_ref, late_mask_ref, early_mask_ref, mixed_ref, sems = refs
    arrivals = fetch(mixed_hbm, mixed_ref, sems)
    shards, rows = out_ref.shape
    spread = late_ref.shape[0] // shards
    late = late_ref.shape[1]
    late_mask = slot_mask(pack_ref[:shards, :], spread).astype(F32)
    early_mask = slot_mask(pack_ref[shards : 2 * shards, :], spread).astype(F32)
    late_mask_ref[...] = late_mask.reshape(late_mask_ref.shape).astype(BF16)
    early_mask_ref[...] = early_mask.reshape(early_mask_ref.shape).astype(BF16)
    flags = flags_of(pack_ref, shards, used)
    for copy in arrivals:
        copy.wait()

    def scored(rows_ref, mixed, mask):
        score = lax.dot_general(
            rows_ref[...], mixed, (((1,), (1,)), ((), ())), preferred_element_type=F32
        )
        score = (score[:, :rows] + score[:, rows:]).reshape(mask.shape)
        return jnp.sum(score * mask, axis=1)

    total = scored(late_ref, mixed_ref[:, :late], late_mask)
    for group, start in chunks_of(early_refs, parts, late):
        lines, each = [], shards // parts
        for i, early_ref in enumerate(group):
            mixed = mixed_ref[:, pl.ds(start, early_ref.shape[1])]
            lines.append(scored(early_ref, mixed, early_mask[i * each : (i + 1) * each]))
        total = total + from_pairs(jnp.concatenate(lines, axis=0), flags)
    out_ref[...] = total


def grad_kernel(
    own_ref, other_ref, pack_ref, late_mask_ref, early_mask_ref, late_ref, *refs, top, used, parts
):
    *early_refs, hidden_ref, out_ref, grad_ref = refs
    layers, rows, features = hidden_ref.shape
    shards = own_ref.shape[0]
    lines = grad_ref.shape[0]
    slots = 128 * ((out_ref.shape[1] - lines) // (2 * top))
    flags = flags_of(pack_ref, shards, used)
    pack = pack_ref[2 * shards + 8 :, :]
    shard, target = pack[:top], pack[top : 2 * top]
    weight, owner, column = [pack[2 * top + i : 2 * top + i + 1] for i in range(3)]
    inverse = pack[2 * top + 3 : 2 * top + 3 + layers]
    inverse = jnp.pad(inverse, ((0, 8 - layers), (0, 0))).T

    by_shard = own_ref[...] + other_ref[...]
    number = iota((shards, rows), 0).astype(F32)
    logits = jnp.concatenate(
        [
            jnp.sum(jnp.where(shard[k : k + 1] == number, by_shard, 0.0), axis=0, keepdims=True)
            for k in range(top)
        ],
        axis=0,
    )
    logits = logits - jnp.max(logits, axis=0, keepdims=True)
    logp = logits - jnp.log(jnp.sum(jnp.exp(logits), axis=0, keepdims=True))
    grad = weight * (jnp.exp(logp) - target)
    by_shard = jnp.zeros((shards, rows), F32)
    for k in range(top):
        by_shard = jnp.where(shard[k : k + 1] == number, grad[k : k + 1], by_shard)

    def spread_out(mask, values):
        mask = mask.astype(F32).reshape(values.shape[0], -1, rows)
        return (mask * values[:, None, :]).reshape(-1, rows).astype(BF16)

    late = late_ref.shape[1]
    pairs = to_pairs(by_shard, flags)
    part = spread_out(early_mask_ref[...], pairs)
    each = part.shape[0] // parts
    part = [part[i * each : (i + 1) * each] for i in range(parts)]
    sources = [([late_ref], [spread_out(late_mask_ref[...], by_shard)], 0)]
    for group, start in chunks_of(early_refs, parts, late):
        sources.append((group, part, start))
    for rows_refs, grads, start in sources:
        for cut in pieces(rows_refs[0].shape[1]):
            carried = sum(
                lax.dot_general(
                    grad, rows_ref[:, cut], (((0,), (0,)), ((), ())), preferred_element_type=F32
                )
                for rows_ref, grad in zip(rows_refs, grads)
            )
            wide, first = carried.shape[1], start + cut.start
            for layer in range(layers):
                scaled = hidden_ref[layer, :, pl.ds(first, wide)].astype(F32)
                scaled = scaled * inverse[:, layer : layer + 1]
                total = jnp.sum(scaled * carried, axis=0, keepdims=True)
                for j in range(wide // 128):
                    line = (layer * features + first) // 128 + j
                    grad_ref[line : line + 1, :] = total[:, j * 128 : (j + 1) * 128]

    high = logp.astype(BF16).astype(F32)
    halves = jnp.concatenate([high, logp - high], axis=0)
    owned = jnp.where(owner == iota((shards, 1, rows), 0).astype(F32), halves[None], 0.0)
    owned = owned.reshape(shards * 2 * top, rows).astype(BF16)
    placed = (iota((slots, rows), 0).astype(F32) == column).astype(BF16)
    sent = lax.dot_general(owned, placed, (((1,), (1,)), ((), ())), preferred_element_type=F32)
    sent = [
        sent[:, j * 128 : (j + 1) * 128].reshape(shards, 2 * top, 128) for j in range(slots // 128)
    ]
    out_ref[:, lines:, :] = jnp.concatenate(sent, axis=1).astype(BF16)
    grad = grad_ref[...].astype(BF16)
    for peer in range(shards):
        out_ref[peer, 0:lines, :] = grad


def sum_kernel(parts_ref, grad_ref, logp_ref):
    total = parts_ref[0].astype(F32)
    for peer in range(1, parts_ref.shape[0]):
        total = total + parts_ref[peer].astype(F32)
    layers, features = grad_ref.shape
    top, slots = logp_ref.shape
    each = features // 128
    for layer in range(layers):
        for j in range(each):
            line = layer * each + j
            grad_ref[layer : layer + 1, j * 128 : (j + 1) * 128] = total[line : line + 1]
    for j in range(slots // 128):
        first = layers * each + j * 2 * top
        logp_ref[:, j * 128 : (j + 1) * 128] = (
            total[first : first + top] + total[first + top : first + 2 * top]
        )


VMEM = pl.BlockSpec(memory_space=pltpu.VMEM)
HBM = pl.BlockSpec(memory_space=pltpu.HBM)


def params():
    return pltpu.CompilerParams(vmem_limit_bytes=VMEM_LIMIT)


def in_hbm(value):
    return pltpu.with_memory_space_constraint(value, pltpu.HBM)


def pick(asked, head, spread, late):
    rows = head.shape[0]
    slots, count = asked.shape[0] // 2 * spread, len(pieces(late))
    return pl.pallas_call(
        functools.partial(pick_kernel, spread=spread),
        in_specs=[VMEM, HBM],
        out_specs=HBM,
        out_shape=pltpu.HBM((slots, late), BF16),
        scratch_shapes=[
            pltpu.VMEM((rows, late), BF16),
            pltpu.VMEM((slots, late), BF16),
            pltpu.SemaphoreType.DMA((count,)),
            pltpu.SemaphoreType.DMA((count,)),
        ],
        compiler_params=params(),
        name="pick",
    )(asked, in_hbm(head))


def begin(group, shard, offset, head, peers, part, starts, wides):
    rows = shard.shape[1]
    return pl.pallas_call(
        functools.partial(begin_kernel, peers=peers, starts=starts),
        in_specs=[pl.BlockSpec(memory_space=pltpu.SMEM), HBM, HBM, HBM],
        out_specs=[HBM] + [VMEM] * len(wides),
        out_shape=[pltpu.HBM((2 * peers, rows), jnp.int32)]
        + [jax.ShapeDtypeStruct((part, wide), BF16) for wide in wides],
        scratch_shapes=[
            pltpu.VMEM(shard.shape, jnp.int32),
            pltpu.VMEM(shard.shape, jnp.int32),
            pltpu.VMEM((2 * peers, rows), jnp.int32),
            pltpu.SemaphoreType.DMA((3 + len(wides),)),
        ],
        compiler_params=params(),
        name="begin",
    )(group.reshape(1), in_hbm(shard), in_hbm(offset), in_hbm(head))


def pick_early(asked, head, near, far, spread, start, count):
    rows, wide = head.shape[0], near.shape[1]
    slots = asked.shape[0] * spread
    return pl.pallas_call(
        functools.partial(early_kernel, spread=spread, start=start),
        in_specs=[VMEM, HBM, VMEM, VMEM],
        out_specs=[VMEM] + [HBM] * (count - 1),
        out_shape=[jax.ShapeDtypeStruct((slots // count, wide), BF16)]
        + [pltpu.HBM((slots // count, wide), BF16)] * (count - 1),
        scratch_shapes=[
            pltpu.VMEM((rows, wide), BF16),
            pltpu.VMEM((max(1, count - 1), slots // count, wide), BF16),
            pltpu.SemaphoreType.DMA((count,)),
        ],
        compiler_params=params(),
        name="pick_early",
    )(asked, in_hbm(head), near, far)


def score(pack, mixed, late, early, shards, used, parts):
    rows = pack.shape[1]
    slots = sum(array.shape[0] for array in early[:parts])
    return pl.pallas_call(
        functools.partial(score_kernel, used=used, parts=parts),
        in_specs=[VMEM, HBM, VMEM] + [VMEM] * len(early),
        out_specs=[VMEM] * 3,
        out_shape=[
            jax.ShapeDtypeStruct((shards, rows), F32),
            jax.ShapeDtypeStruct((late.shape[0], rows), BF16),
            jax.ShapeDtypeStruct((slots, rows), BF16),
        ],
        scratch_shapes=[
            pltpu.VMEM(mixed.shape, BF16),
            pltpu.SemaphoreType.DMA((len(pieces(mixed.shape[1])),)),
        ],
        compiler_params=params(),
        name="score",
    )(pack, in_hbm(mixed), late, *early)


def gradient(own, other, pack, masks, late, early, hidden, lines, total_lines, top, used, parts):
    return pl.pallas_call(
        functools.partial(grad_kernel, top=top, used=used, parts=parts),
        in_specs=[VMEM] * (7 + len(early)),
        out_specs=VMEM,
        out_shape=jax.ShapeDtypeStruct((own.shape[0], total_lines, 128), BF16),
        scratch_shapes=[
            pltpu.VMEM((lines, 128), F32),
        ],
        compiler_params=params(),
        name="gradient",
    )(own, other, pack, *masks, late, *early, hidden)


def after(value, first):
    return lax.optimization_barrier((value, first))[0]


def add_up(parts, layers, features, top, slots):
    return pl.pallas_call(
        sum_kernel,
        in_specs=[VMEM],
        out_specs=[VMEM] * 2,
        out_shape=[
            jax.ShapeDtypeStruct((layers, features), F32),
            jax.ShapeDtypeStruct((top, slots), F32),
        ],
        compiler_params=params(),
        name="add_up",
    )(parts)


def rounded(value):
    return lax.reduce_precision(value, exponent_bits=8, mantissa_bits=7)


def position_weights(lengths, positions, sequences):
    seq_ends = jnp.cumsum(lengths)
    seq_starts = seq_ends - lengths
    position = jnp.arange(positions, dtype=jnp.int32)[None, :]
    member = (position >= seq_starts[:, None]) & (position < seq_ends[:, None])
    own_length = jnp.sum(jnp.where(member, lengths[:, None], 0), axis=0, keepdims=True)
    closing = jnp.any(member & (position == seq_ends[:, None] - 1), axis=0, keepdims=True)
    portion = 1.0 / (own_length.astype(F32) * sequences)
    return rounded(jnp.where(closing, 0.0, portion))


def swap_cores(value):
    size = lax.axis_size("mp")
    if size == 1:
        return jnp.zeros_like(value)
    return lax.ppermute(value, "mp", [(i, i ^ 1) for i in range(size)])


def exchange(value, groups=None):
    return lax.all_to_all(
        value, "dp", split_axis=0, concat_axis=0, tiled=True, axis_index_groups=groups
    )


def local(
    hidden,
    row_owner,
    candidate_shard,
    candidate_offset,
    target_logits,
    lengths,
    layer_mix,
    draft_head,
):
    rows, layers, features = hidden.shape
    top = candidate_shard.shape[1]
    peers = lax.axis_size("dp")
    cores = lax.axis_size("mp")
    capacity = max(2, 2 * rows // peers)
    spread = min(rows, max(2, 3 * rows * top // (2 * peers)))
    spread = -(-spread // 16) * 16
    half = peers // 2
    late = features - sum(CHUNKS) * features // 2048
    place, group = lax.axis_index("dp"), lax.axis_index("groups")

    count = draft_head.shape[0]
    part = count // 2
    wides = [wide * features // 2048 for wide in CHUNKS]
    starts = [late + sum(wides[:i]) for i in range(len(wides))]
    shard, offset = candidate_shard.T, candidate_offset.T
    message, *slices = begin(group, shard, offset, draft_head, peers, part, starts, wides)
    across = [(i, (i + half) % peers) for i in range(peers)]
    chunks = [(start, lax.ppermute(near, "dp", across)) for start, near in zip(starts, slices)]
    wanted = exchange(message.reshape(peers, 2, rows)).reshape(2 * peers, rows)

    picked = pick(wanted, draft_head, spread, late)
    rows_late = exchange(picked.reshape(peers, spread, late)).reshape(peers * spread, late)

    few = half <= 4
    parts = half if few else 1
    bits = [b for b in range(peers.bit_length() - 1) if few or 1 << b == half]
    used = [b in bits for b in range(peers.bit_length() - 1)]
    flags = [(place >> b) & 1 if use else None for b, use in enumerate(used)]
    wanted = lax.dynamic_slice(wanted, (place // half * half * 2, 0), (half * 2, rows))
    wanted = swapped(wanted, [None] + [None if flag is None else flag > 0 for flag in flags[:-1]])
    rows_early = []
    for start, near in chunks:
        near = after(near, picked)
        far = lax.ppermute(near, "groups", [(0, 1), (1, 0)])
        rows_here = list(pick_early(wanted, draft_head, near, far, spread, start, parts))
        if few:
            for i in range(1, half):
                rows_here[i] = lax.ppermute(rows_here[i], "dp", [(j, j ^ i) for j in range(peers)])
        else:
            halves = [list(range(half)), list(range(half, peers))]
            rows_here = exchange(rows_here[0].reshape(half, 2 * spread, -1), halves)
            rows_here = [rows_here.reshape(peers * spread, -1)]
        rows_early += rows_here

    number = jnp.arange(peers, dtype=jnp.int32)[:, None]
    asked = jnp.max(
        jnp.where(shard[:, None, :] == number[None], offset[:, None, :], -1), axis=0
    )
    tokens = hidden.transpose(1, 0, 2)
    wide = tokens.astype(F32)
    squares = jnp.sum(wide * wide, axis=2)
    squares = squares + swap_cores(squares)
    inverse = lax.rsqrt(squares / (features * cores) + EPS)
    mixed = jnp.sum(wide * layer_mix[:, None, :] * inverse[:, :, None], axis=0)
    high = rounded(mixed)
    mixed = jnp.concatenate([high, mixed - high], axis=0).astype(BF16)

    weight = position_weights(lengths[0], rows, float(lengths.shape[1] * peers))
    target = jax.nn.softmax(target_logits.T.astype(F32), axis=0)
    owner = row_owner.T
    same = (owner.T == owner) & (iota((rows, rows), 1) < iota((rows, rows), 0))
    column = lax.axis_index("dp") * capacity + jnp.sum(same.astype(jnp.int32), axis=1)[None, :]
    held = [jnp.full((1, rows), 0 if flag is None else flag, jnp.int32) for flag in flags]
    held = jnp.pad(jnp.concatenate(held, axis=0), ((0, 8 - len(held)), (0, 0)))
    pairs = to_pairs(asked, [None if flag is None else flag > 0 for flag in flags])
    pack = [asked, pairs, held, shard, target, weight, owner, column, inverse]
    pack = jnp.concatenate([value.astype(F32) for value in pack], axis=0)
    pack = jnp.pad(pack, ((0, -pack.shape[0] % 8), (0, 0)))

    slots = peers * capacity
    lines = layers * features // 128
    total_lines = lines + 2 * top * slots // 128
    own, *masks = score(pack, mixed, rows_late, rows_early, peers, used, parts)
    other = swap_cores(own)
    sent = gradient(
        own, other, pack, masks, rows_late, rows_early, tokens, lines, total_lines, top, used, parts
    )
    grad, logp = add_up(exchange(sent), layers, features, top, slots)
    return (logp.T[None], grad)


def solution(mesh):
    return jax.shard_map(
        local,
        mesh=mesh,
        in_specs=(
            P(("groups", "dp"), None, "mp"),
            P(("groups", "dp"), None),
            P(("groups", "dp"), None),
            P(("groups", "dp"), None),
            P(("groups", "dp"), None),
            P(("groups", "dp"), None),
            P(None, "mp"),
            P("dp", "mp"),
        ),
        out_specs=(P(("groups", "dp"), None, None), P("groups", "mp")),
        check_vma=False,
    )
```

```python
import functools

import jax
import jax.numpy as jnp
from jax import lax
from jax.experimental import pallas as pl
from jax.experimental.pallas import tpu as pltpu
from jax.sharding import PartitionSpec as P

EPS = 1e-06
HIGHEST = lax.Precision.HIGHEST
F32 = jnp.float32
BF16 = jnp.bfloat16
VMEM_LIMIT = 16 * 1024 * 1024
CHUNKS = (384, 256)


def iota(shape, axis):
    return lax.broadcasted_iota(jnp.int32, shape, axis)


def slot_mask(asked, spread):
    shards, rows = asked.shape
    held = asked >= 0
    earlier = (iota((rows, rows), 0) < iota((rows, rows), 1)).astype(BF16)
    rank = jnp.dot(held.astype(BF16), earlier, preferred_element_type=F32)
    rank = jnp.where(held, rank, -1.0)
    place = iota((shards, spread, rows), 1).astype(F32)
    return rank[:, None, :] == place


def pieces(features):
    return [pl.ds(start, min(512, features - start)) for start in range(0, features, 512)]


def fetch(source, target, sems):
    lead = (slice(None),) * (len(source.shape) - 1)
    copies = [
        pltpu.make_async_copy(source.at[(*lead, cut)], target.at[(*lead, cut)], sems.at[i])
        for i, cut in enumerate(pieces(source.shape[-1]))
    ]
    for copy in copies:
        copy.start()
    return copies


def hot_rows(asked, spread, count):
    shards, rows = asked.shape
    mask = slot_mask(asked, spread)
    row = jnp.where(mask, (asked.astype(F32) + 1.0)[:, None, :], 0.0)
    row = jnp.sum(row.reshape(shards * spread, rows), axis=1, keepdims=True) - 1.0
    return jnp.where(row == iota((1, count), 1).astype(F32), 1.0, 0.0).astype(BF16)


def every_other(ref, first):
    lines = [ref[i : i + 1, :] for i in range(first, ref.shape[0], 2)]
    return jnp.concatenate(lines, axis=0)


def pick_kernel(asked_ref, head_hbm, out_hbm, head_ref, picked_ref, in_sems, out_sems, *, spread):
    late = head_ref.shape[1]
    arrivals = fetch(head_hbm.at[:, :late], head_ref, in_sems)
    hot = hot_rows(every_other(asked_ref, 0), spread, head_ref.shape[0])
    departures = []
    for i, cut in enumerate(pieces(late)):
        arrivals[i].wait()
        picked_ref[:, cut] = jnp.dot(
            hot, head_ref[:, cut], preferred_element_type=F32
        ).astype(BF16)
        copy = pltpu.make_async_copy(picked_ref.at[:, cut], out_hbm.at[:, cut], out_sems.at[i])
        copy.start()
        departures.append(copy)
    for copy in departures:
        copy.wait()


def begin_kernel(
    group_ref, shard_hbm, offset_hbm, head_hbm, message_hbm, *refs, peers, starts
):
    *out_refs, shard_ref, offset_ref, message_ref, sems = refs
    small = [
        pltpu.make_async_copy(shard_hbm, shard_ref, sems.at[0]),
        pltpu.make_async_copy(offset_hbm, offset_ref, sems.at[1]),
    ]
    large = []
    part = out_refs[0].shape[0]
    shift = group_ref[0] * part
    for i, out_ref in enumerate(out_refs):
        rows = pl.ds(pl.multiple_of(shift, part), part)
        source = head_hbm.at[rows, pl.ds(starts[i], out_ref.shape[1])]
        large.append(pltpu.make_async_copy(source, out_ref, sems.at[3 + i]))
    for copy in small + large:
        copy.start()
    for copy in small:
        copy.wait()
    shard, offset = shard_ref[...], offset_ref[...]
    count = head_hbm.shape[0]
    other = offset + shift
    other = jnp.where(other >= count, other - count, other)
    line = iota(message_ref.shape, 0)
    number = line // 2 + jnp.where(line % 2 == 0, 0, peers // 2)
    number = jnp.where(number >= peers, number - peers, number)
    message = jnp.full(message_ref.shape, -1, jnp.int32)
    for k in range(shard.shape[0]):
        asked = jnp.where(line % 2 == 0, offset[k : k + 1], other[k : k + 1])
        message = jnp.where(shard[k : k + 1] == number, asked, message)
    message_ref[...] = message
    copy = pltpu.make_async_copy(message_ref, message_hbm, sems.at[2])
    copy.start()
    copy.wait()
    for copy in large:
        copy.wait()


def early_kernel(asked_ref, head_hbm, near_ref, far_ref, *refs, spread, start):
    *out_refs, own_ref, sent_ref, sems = refs
    count, wide = own_ref.shape
    copy = pltpu.make_async_copy(head_hbm.at[:, pl.ds(start, wide)], own_ref, sems.at[0])
    copy.start()
    peers = asked_ref.shape[0] // 2
    hot = [hot_rows(every_other(asked_ref, i), spread, count) for i in range(2)]
    other = sum(
        jnp.dot(
            hot[1][:, j * count // 2 : (j + 1) * count // 2],
            ref[...],
            preferred_element_type=F32,
        )
        for j, ref in enumerate((near_ref, far_ref))
    )
    copy.wait()
    own = jnp.dot(hot[0], own_ref[...], preferred_element_type=F32)
    each = 2 * peers * spread // len(out_refs)
    targets = [out_refs[0]] + [sent_ref.at[i] for i in range(len(out_refs) - 1)]
    for i, picked in enumerate((own.astype(BF16), other.astype(BF16))):
        for peer in range(peers):
            first = (2 * peer + i) * spread
            targets[first // each][first % each : first % each + spread, :] = picked[
                peer * spread : (peer + 1) * spread
            ]
    copies = [
        pltpu.make_async_copy(sent_ref.at[i], out_ref, sems.at[1 + i])
        for i, out_ref in enumerate(out_refs[1:])
    ]
    for copy in copies:
        copy.start()
    for copy in copies:
        copy.wait()


def swapped(value, flags):
    size = value.shape[0]
    for bit, flag in enumerate(flags):
        if flag is None:
            continue
        step = 1 << bit
        other = [value[start ^ step : (start ^ step) + step] for start in range(0, size, step)]
        value = jnp.where(flag, jnp.concatenate(other, axis=0), value)
    return value


def to_pairs(value, flags):
    half = value.shape[0] // 2
    value = swapped(value, flags)
    lines = [value[j * half + i : j * half + i + 1] for i in range(half) for j in range(2)]
    return jnp.concatenate(lines, axis=0)


def from_pairs(value, flags):
    size = value.shape[0]
    lines = [value[i : i + 1] for j in range(2) for i in range(j, size, 2)]
    return swapped(jnp.concatenate(lines, axis=0), flags)


def flags_of(pack_ref, shards, used):
    lines = pack_ref[2 * shards : 2 * shards + 8, :]
    return [lines[b : b + 1] > 0.5 if use else None for b, use in enumerate(used)]


def chunks_of(refs, parts, start):
    for i in range(0, len(refs), parts):
        yield refs[i : i + parts], start
        start += refs[i].shape[1]


def slot_sums(fetched, mixed, mask):
    rows = mask.shape[2]
    score = lax.dot_general(
        fetched, mixed, (((1,), (1,)), ((), ())), preferred_element_type=F32
    )
    score = (score[:, :rows] + score[:, rows:]).reshape(mask.shape)
    return jnp.sum(score * mask, axis=1)


def early_score_kernel(pack_ref, mixed_hbm, *refs, used, parts):
    *early_refs, out_ref, mixed_ref, sem = refs
    shards = out_ref.shape[0]
    wide = mixed_ref.shape[1]
    late = mixed_hbm.shape[1] - wide
    copy = pltpu.make_async_copy(mixed_hbm.at[:, pl.ds(late, wide)], mixed_ref, sem)
    copy.start()
    each = shards // parts
    mask = slot_mask(pack_ref[shards : 2 * shards, :], early_refs[0].shape[0] // each).astype(F32)
    copy.wait()
    lines = [0.0] * parts
    for group, start in chunks_of(early_refs, parts, 0):
        for i, early_ref in enumerate(group):
            mixed = mixed_ref[:, pl.ds(start, early_ref.shape[1])]
            lines[i] += slot_sums(early_ref[...], mixed, mask[i * each : (i + 1) * each])
    out_ref[...] = from_pairs(jnp.concatenate(lines, axis=0), flags_of(pack_ref, shards, used))


def score_kernel(pack_ref, early_ref, mixed_hbm, late_ref, out_ref, mask_ref, mixed_ref, sem):
    shards = out_ref.shape[0]
    copy = pltpu.make_async_copy(mixed_hbm.at[:, pl.ds(0, late_ref.shape[1])], mixed_ref, sem)
    copy.start()
    mask = slot_mask(pack_ref[:shards, :], late_ref.shape[0] // shards).astype(F32)
    mask_ref[...] = mask.reshape(mask_ref.shape).astype(BF16)
    copy.wait()
    out_ref[...] = slot_sums(late_ref[...], mixed_ref[...], mask) + early_ref[...]


def grad_kernel(
    own_ref, other_ref, pack_ref, late_mask_ref, late_ref, *refs, top, used, parts
):
    *early_refs, hidden_ref, out_ref, grad_ref = refs
    layers, rows, features = hidden_ref.shape
    shards = own_ref.shape[0]
    lines = grad_ref.shape[0]
    slots = 128 * ((out_ref.shape[1] - lines) // (2 * top))
    flags = flags_of(pack_ref, shards, used)
    pack = pack_ref[2 * shards + 8 :, :]
    shard, target = pack[:top], pack[top : 2 * top]
    weight, owner, column = [pack[2 * top + i : 2 * top + i + 1] for i in range(3)]
    inverse = pack[2 * top + 3 : 2 * top + 3 + layers]
    inverse = jnp.pad(inverse, ((0, 8 - layers), (0, 0))).T

    by_shard = own_ref[...] + other_ref[...]
    number = iota((shards, rows), 0).astype(F32)
    logits = jnp.concatenate(
        [
            jnp.sum(jnp.where(shard[k : k + 1] == number, by_shard, 0.0), axis=0, keepdims=True)
            for k in range(top)
        ],
        axis=0,
    )
    logits = logits - jnp.max(logits, axis=0, keepdims=True)
    logp = logits - jnp.log(jnp.sum(jnp.exp(logits), axis=0, keepdims=True))
    grad = weight * (jnp.exp(logp) - target)
    by_shard = jnp.zeros((shards, rows), F32)
    for k in range(top):
        by_shard = jnp.where(shard[k : k + 1] == number, grad[k : k + 1], by_shard)

    def spread_out(mask, values):
        mask = mask.astype(F32).reshape(values.shape[0], -1, rows)
        return (mask * values[:, None, :]).reshape(-1, rows).astype(BF16)

    late = late_ref.shape[1]
    pairs = to_pairs(by_shard, flags)
    spread = late_mask_ref.shape[0] // shards
    early_mask = slot_mask(pack_ref[shards : 2 * shards, :], spread)
    part = spread_out(early_mask, pairs)
    each = part.shape[0] // parts
    part = [part[i * each : (i + 1) * each] for i in range(parts)]
    sources = [([late_ref], [spread_out(late_mask_ref[...], by_shard)], 0)]
    for group, start in chunks_of(early_refs, parts, late):
        sources.append((group, part, start))
    for rows_refs, grads, start in sources:
        for cut in pieces(rows_refs[0].shape[1]):
            carried = sum(
                lax.dot_general(
                    grad, rows_ref[:, cut], (((0,), (0,)), ((), ())), preferred_element_type=F32
                )
                for rows_ref, grad in zip(rows_refs, grads)
            )
            wide, first = carried.shape[1], start + cut.start
            for layer in range(layers):
                scaled = hidden_ref[layer, :, pl.ds(first, wide)].astype(F32)
                scaled = scaled * inverse[:, layer : layer + 1]
                total = jnp.sum(scaled * carried, axis=0, keepdims=True)
                for j in range(wide // 128):
                    line = (layer * features + first) // 128 + j
                    grad_ref[line : line + 1, :] = total[:, j * 128 : (j + 1) * 128]

    high = logp.astype(BF16).astype(F32)
    halves = jnp.concatenate([high, logp - high], axis=0)
    owned = jnp.where(owner == iota((shards, 1, rows), 0).astype(F32), halves[None], 0.0)
    owned = owned.reshape(shards * 2 * top, rows).astype(BF16)
    placed = (iota((slots, rows), 0).astype(F32) == column).astype(BF16)
    sent = lax.dot_general(owned, placed, (((1,), (1,)), ((), ())), preferred_element_type=F32)
    sent = [
        sent[:, j * 128 : (j + 1) * 128].reshape(shards, 2 * top, 128) for j in range(slots // 128)
    ]
    out_ref[:, lines:, :] = jnp.concatenate(sent, axis=1).astype(BF16)
    grad = grad_ref[...].astype(BF16)
    for peer in range(shards):
        out_ref[peer, 0:lines, :] = grad


def sum_kernel(parts_ref, grad_ref, logp_ref):
    total = parts_ref[0].astype(F32)
    for peer in range(1, parts_ref.shape[0]):
        total = total + parts_ref[peer].astype(F32)
    layers, features = grad_ref.shape
    top, slots = logp_ref.shape
    each = features // 128
    for layer in range(layers):
        for j in range(each):
            line = layer * each + j
            grad_ref[layer : layer + 1, j * 128 : (j + 1) * 128] = total[line : line + 1]
    for j in range(slots // 128):
        first = layers * each + j * 2 * top
        logp_ref[:, j * 128 : (j + 1) * 128] = (
            total[first : first + top] + total[first + top : first + 2 * top]
        )


VMEM = pl.BlockSpec(memory_space=pltpu.VMEM)
HBM = pl.BlockSpec(memory_space=pltpu.HBM)


def params():
    return pltpu.CompilerParams(vmem_limit_bytes=VMEM_LIMIT)


def in_hbm(value):
    return pltpu.with_memory_space_constraint(value, pltpu.HBM)


def pick(asked, head, spread, late):
    rows = head.shape[0]
    slots, count = asked.shape[0] // 2 * spread, len(pieces(late))
    return pl.pallas_call(
        functools.partial(pick_kernel, spread=spread),
        in_specs=[VMEM, HBM],
        out_specs=HBM,
        out_shape=pltpu.HBM((slots, late), BF16),
        scratch_shapes=[
            pltpu.VMEM((rows, late), BF16),
            pltpu.VMEM((slots, late), BF16),
            pltpu.SemaphoreType.DMA((count,)),
            pltpu.SemaphoreType.DMA((count,)),
        ],
        compiler_params=params(),
        name="pick",
    )(asked, in_hbm(head))


def begin(group, shard, offset, head, peers, part, starts, wides):
    rows = shard.shape[1]
    return pl.pallas_call(
        functools.partial(begin_kernel, peers=peers, starts=starts),
        in_specs=[pl.BlockSpec(memory_space=pltpu.SMEM), HBM, HBM, HBM],
        out_specs=[HBM] + [VMEM] * len(wides),
        out_shape=[pltpu.HBM((2 * peers, rows), jnp.int32)]
        + [jax.ShapeDtypeStruct((part, wide), BF16) for wide in wides],
        scratch_shapes=[
            pltpu.VMEM(shard.shape, jnp.int32),
            pltpu.VMEM(shard.shape, jnp.int32),
            pltpu.VMEM((2 * peers, rows), jnp.int32),
            pltpu.SemaphoreType.DMA((3 + len(wides),)),
        ],
        compiler_params=params(),
        name="begin",
    )(group.reshape(1), in_hbm(shard), in_hbm(offset), in_hbm(head))


def pick_early(asked, head, near, far, spread, start, count):
    rows, wide = head.shape[0], near.shape[1]
    slots = asked.shape[0] * spread
    return pl.pallas_call(
        functools.partial(early_kernel, spread=spread, start=start),
        in_specs=[VMEM, HBM, VMEM, VMEM],
        out_specs=[VMEM] + [HBM] * (count - 1),
        out_shape=[jax.ShapeDtypeStruct((slots // count, wide), BF16)]
        + [pltpu.HBM((slots // count, wide), BF16)] * (count - 1),
        scratch_shapes=[
            pltpu.VMEM((rows, wide), BF16),
            pltpu.VMEM((max(1, count - 1), slots // count, wide), BF16),
            pltpu.SemaphoreType.DMA((count,)),
        ],
        compiler_params=params(),
        name="pick_early",
    )(asked, in_hbm(head), near, far)


def score_early(pack, mixed, early, shards, used, parts):
    rows = pack.shape[1]
    wide = sum(array.shape[1] for array in early[::parts])
    return pl.pallas_call(
        functools.partial(early_score_kernel, used=used, parts=parts),
        in_specs=[VMEM, HBM] + [VMEM] * len(early),
        out_specs=VMEM,
        out_shape=jax.ShapeDtypeStruct((shards, rows), F32),
        scratch_shapes=[pltpu.VMEM((mixed.shape[0], wide), BF16), pltpu.SemaphoreType.DMA(())],
        compiler_params=params(),
        name="score_early",
    )(pack, in_hbm(mixed), *early)


def score(pack, early, mixed, late, shards):
    rows = pack.shape[1]
    return pl.pallas_call(
        score_kernel,
        in_specs=[VMEM, VMEM, HBM, VMEM],
        out_specs=[VMEM] * 2,
        out_shape=[
            jax.ShapeDtypeStruct((shards, rows), F32),
            jax.ShapeDtypeStruct((late.shape[0], rows), BF16),
        ],
        scratch_shapes=[
            pltpu.VMEM((mixed.shape[0], late.shape[1]), BF16),
            pltpu.SemaphoreType.DMA(()),
        ],
        compiler_params=params(),
        name="score",
    )(pack, early, in_hbm(mixed), late)


def gradient(own, other, pack, mask, late, early, hidden, lines, total_lines, top, used, parts):
    return pl.pallas_call(
        functools.partial(grad_kernel, top=top, used=used, parts=parts),
        in_specs=[VMEM] * (6 + len(early)),
        out_specs=VMEM,
        out_shape=jax.ShapeDtypeStruct((own.shape[0], total_lines, 128), BF16),
        scratch_shapes=[
            pltpu.VMEM((lines, 128), F32),
        ],
        compiler_params=params(),
        name="gradient",
    )(own, other, pack, mask, late, *early, hidden)


def after(value, first):
    return lax.optimization_barrier((value, first))[0]


def add_up(parts, layers, features, top, slots):
    return pl.pallas_call(
        sum_kernel,
        in_specs=[VMEM],
        out_specs=[VMEM] * 2,
        out_shape=[
            jax.ShapeDtypeStruct((layers, features), F32),
            jax.ShapeDtypeStruct((top, slots), F32),
        ],
        compiler_params=params(),
        name="add_up",
    )(parts)


def rounded(value):
    return lax.reduce_precision(value, exponent_bits=8, mantissa_bits=7)


def position_weights(lengths, positions, sequences):
    seq_ends = jnp.cumsum(lengths)
    seq_starts = seq_ends - lengths
    position = jnp.arange(positions, dtype=jnp.int32)[None, :]
    member = (position >= seq_starts[:, None]) & (position < seq_ends[:, None])
    own_length = jnp.sum(jnp.where(member, lengths[:, None], 0), axis=0, keepdims=True)
    closing = jnp.any(member & (position == seq_ends[:, None] - 1), axis=0, keepdims=True)
    portion = 1.0 / (own_length.astype(F32) * sequences)
    return rounded(jnp.where(closing, 0.0, portion))


def swap_cores(value):
    size = lax.axis_size("mp")
    if size == 1:
        return jnp.zeros_like(value)
    return lax.ppermute(value, "mp", [(i, i ^ 1) for i in range(size)])


def exchange(value, groups=None):
    return lax.all_to_all(
        value, "dp", split_axis=0, concat_axis=0, tiled=True, axis_index_groups=groups
    )


def local(
    hidden,
    row_owner,
    candidate_shard,
    candidate_offset,
    target_logits,
    lengths,
    layer_mix,
    draft_head,
):
    rows, layers, features = hidden.shape
    top = candidate_shard.shape[1]
    peers = lax.axis_size("dp")
    cores = lax.axis_size("mp")
    capacity = max(2, 2 * rows // peers)
    spread = min(rows, max(2, 3 * rows * top // (2 * peers)))
    spread = -(-spread // 16) * 16
    half = peers // 2
    late = features - sum(CHUNKS) * features // 2048
    place, group = lax.axis_index("dp"), lax.axis_index("groups")

    count = draft_head.shape[0]
    part = count // 2
    wides = [wide * features // 2048 for wide in CHUNKS]
    starts = [late + sum(wides[:i]) for i in range(len(wides))]
    shard, offset = candidate_shard.T, candidate_offset.T
    message, *slices = begin(group, shard, offset, draft_head, peers, part, starts, wides)
    across = [(i, (i + half) % peers) for i in range(peers)]
    chunks = [(start, lax.ppermute(near, "dp", across)) for start, near in zip(starts, slices)]
    wanted = exchange(message.reshape(peers, 2, rows)).reshape(2 * peers, rows)

    picked = pick(wanted, draft_head, spread, late)
    rows_late = exchange(picked.reshape(peers, spread, late)).reshape(peers * spread, late)

    few = half <= 4
    parts = half if few else 1
    bits = [b for b in range(peers.bit_length() - 1) if few or 1 << b == half]
    used = [b in bits for b in range(peers.bit_length() - 1)]
    flags = [(place >> b) & 1 if use else None for b, use in enumerate(used)]
    wanted = lax.dynamic_slice(wanted, (place // half * half * 2, 0), (half * 2, rows))
    wanted = swapped(wanted, [None] + [None if flag is None else flag > 0 for flag in flags[:-1]])
    rows_early = []
    for start, near in chunks:
        near = after(near, picked)
        far = lax.ppermute(near, "groups", [(0, 1), (1, 0)])
        rows_here = list(pick_early(wanted, draft_head, near, far, spread, start, parts))
        if few:
            for i in range(1, half):
                rows_here[i] = lax.ppermute(rows_here[i], "dp", [(j, j ^ i) for j in range(peers)])
        else:
            halves = [list(range(half)), list(range(half, peers))]
            rows_here = exchange(rows_here[0].reshape(half, 2 * spread, -1), halves)
            rows_here = [rows_here.reshape(peers * spread, -1)]
        rows_early += rows_here

    hidden, layer_mix = after((hidden, layer_mix), picked)
    number = jnp.arange(peers, dtype=jnp.int32)[:, None]
    asked = jnp.max(
        jnp.where(shard[:, None, :] == number[None], offset[:, None, :], -1), axis=0
    )
    tokens = hidden.transpose(1, 0, 2)
    wide = tokens.astype(F32)
    squares = jnp.sum(wide * wide, axis=2)
    squares = squares + swap_cores(squares)
    inverse = lax.rsqrt(squares / (features * cores) + EPS)
    mixed = jnp.sum(wide * layer_mix[:, None, :] * inverse[:, :, None], axis=0)
    high = rounded(mixed)
    mixed = jnp.concatenate([high, mixed - high], axis=0).astype(BF16)

    weight = position_weights(lengths[0], rows, float(lengths.shape[1] * peers))
    target = jax.nn.softmax(target_logits.T.astype(F32), axis=0)
    owner = row_owner.T
    same = (owner.T == owner) & (iota((rows, rows), 1) < iota((rows, rows), 0))
    column = lax.axis_index("dp") * capacity + jnp.sum(same.astype(jnp.int32), axis=1)[None, :]
    held = [jnp.full((1, rows), 0 if flag is None else flag, jnp.int32) for flag in flags]
    held = jnp.pad(jnp.concatenate(held, axis=0), ((0, 8 - len(held)), (0, 0)))
    pairs = to_pairs(asked, [None if flag is None else flag > 0 for flag in flags])
    pack = [asked, pairs, held, shard, target, weight, owner, column, inverse]
    pack = jnp.concatenate([value.astype(F32) for value in pack], axis=0)
    pack = jnp.pad(pack, ((0, -pack.shape[0] % 8), (0, 0)))

    slots = peers * capacity
    lines = layers * features // 128
    total_lines = lines + 2 * top * slots // 128
    early = score_early(pack, mixed, rows_early, peers, used, parts)
    own, mask = score(pack, early, mixed, rows_late, peers)
    other = swap_cores(own)
    sent = gradient(
        own, other, pack, mask, rows_late, rows_early, tokens, lines, total_lines, top, used, parts
    )
    grad, logp = add_up(exchange(sent), layers, features, top, slots)
    return (logp.T[None], grad)


def solution(mesh):
    return jax.shard_map(
        local,
        mesh=mesh,
        in_specs=(
            P(("groups", "dp"), None, "mp"),
            P(("groups", "dp"), None),
            P(("groups", "dp"), None),
            P(("groups", "dp"), None),
            P(("groups", "dp"), None),
            P(("groups", "dp"), None),
            P(None, "mp"),
            P("dp", "mp"),
        ),
        out_specs=(P(("groups", "dp"), None, None), P("groups", "mp")),
        check_vma=False,
    )
```

```python
import functools

import jax
import jax.numpy as jnp
from jax import lax
from jax.experimental import pallas as pl
from jax.experimental.pallas import tpu as pltpu
from jax.sharding import PartitionSpec as P

EPS = 1e-06
HIGHEST = lax.Precision.HIGHEST
F32 = jnp.float32
BF16 = jnp.bfloat16
VMEM_LIMIT = 16 * 1024 * 1024
CHUNKS = (256, 384)


def iota(shape, axis):
    return lax.broadcasted_iota(jnp.int32, shape, axis)


def slot_mask(asked, spread):
    shards, rows = asked.shape
    held = asked >= 0
    earlier = (iota((rows, rows), 0) < iota((rows, rows), 1)).astype(BF16)
    rank = jnp.dot(held.astype(BF16), earlier, preferred_element_type=F32)
    rank = jnp.where(held, rank, -1.0)
    place = iota((shards, spread, rows), 1).astype(F32)
    return rank[:, None, :] == place


def pieces(features):
    return [pl.ds(start, min(512, features - start)) for start in range(0, features, 512)]


def fetch(source, target, sems):
    lead = (slice(None),) * (len(source.shape) - 1)
    copies = [
        pltpu.make_async_copy(source.at[(*lead, cut)], target.at[(*lead, cut)], sems.at[i])
        for i, cut in enumerate(pieces(source.shape[-1]))
    ]
    for copy in copies:
        copy.start()
    return copies


def hot_rows(asked, spread, count):
    shards, rows = asked.shape
    mask = slot_mask(asked, spread)
    row = jnp.where(mask, (asked.astype(F32) + 1.0)[:, None, :], 0.0)
    row = jnp.sum(row.reshape(shards * spread, rows), axis=1, keepdims=True) - 1.0
    return jnp.where(row == iota((1, count), 1).astype(F32), 1.0, 0.0).astype(BF16)


def every_other(ref, first):
    lines = [ref[i : i + 1, :] for i in range(first, ref.shape[0], 2)]
    return jnp.concatenate(lines, axis=0)


def pick_kernel(asked_ref, head_hbm, out_hbm, head_ref, picked_ref, in_sems, out_sems, *, spread):
    late = head_ref.shape[1]
    arrivals = fetch(head_hbm.at[:, :late], head_ref, in_sems)
    hot = hot_rows(every_other(asked_ref, 0), spread, head_ref.shape[0])
    departures = []
    for i, cut in enumerate(pieces(late)):
        arrivals[i].wait()
        picked_ref[:, cut] = jnp.dot(
            hot, head_ref[:, cut], preferred_element_type=F32
        ).astype(BF16)
        copy = pltpu.make_async_copy(picked_ref.at[:, cut], out_hbm.at[:, cut], out_sems.at[i])
        copy.start()
        departures.append(copy)
    for copy in departures:
        copy.wait()


def begin_kernel(
    group_ref, shard_hbm, offset_hbm, head_hbm, message_hbm, *refs, peers, starts
):
    *out_refs, shard_ref, offset_ref, message_ref, sems = refs
    small = [
        pltpu.make_async_copy(shard_hbm, shard_ref, sems.at[0]),
        pltpu.make_async_copy(offset_hbm, offset_ref, sems.at[1]),
    ]
    large = []
    part = out_refs[0].shape[0]
    shift = group_ref[0] * part
    for i, out_ref in enumerate(out_refs):
        rows = pl.ds(pl.multiple_of(shift, part), part)
        source = head_hbm.at[rows, pl.ds(starts[i], out_ref.shape[1])]
        large.append(pltpu.make_async_copy(source, out_ref, sems.at[3 + i]))
    for copy in small + large:
        copy.start()
    for copy in small:
        copy.wait()
    shard, offset = shard_ref[...], offset_ref[...]
    count = head_hbm.shape[0]
    other = offset + shift
    other = jnp.where(other >= count, other - count, other)
    line = iota(message_ref.shape, 0)
    number = line // 2 + jnp.where(line % 2 == 0, 0, peers // 2)
    number = jnp.where(number >= peers, number - peers, number)
    message = jnp.full(message_ref.shape, -1, jnp.int32)
    for k in range(shard.shape[0]):
        asked = jnp.where(line % 2 == 0, offset[k : k + 1], other[k : k + 1])
        message = jnp.where(shard[k : k + 1] == number, asked, message)
    message_ref[...] = message
    copy = pltpu.make_async_copy(message_ref, message_hbm, sems.at[2])
    copy.start()
    copy.wait()
    for copy in large:
        copy.wait()


def early_kernel(asked_ref, head_hbm, near_ref, far_ref, *refs, spread, start):
    *out_refs, own_ref, sent_ref, sems = refs
    count, wide = own_ref.shape
    copy = pltpu.make_async_copy(head_hbm.at[:, pl.ds(start, wide)], own_ref, sems.at[0])
    copy.start()
    peers = asked_ref.shape[0] // 2
    hot = [hot_rows(every_other(asked_ref, i), spread, count) for i in range(2)]
    other = sum(
        jnp.dot(
            hot[1][:, j * count // 2 : (j + 1) * count // 2],
            ref[...],
            preferred_element_type=F32,
        )
        for j, ref in enumerate((near_ref, far_ref))
    )
    copy.wait()
    own = jnp.dot(hot[0], own_ref[...], preferred_element_type=F32)
    each = 2 * peers * spread // len(out_refs)
    targets = [out_refs[0]] + [sent_ref.at[i] for i in range(len(out_refs) - 1)]
    for i, picked in enumerate((own.astype(BF16), other.astype(BF16))):
        for peer in range(peers):
            first = (2 * peer + i) * spread
            targets[first // each][first % each : first % each + spread, :] = picked[
                peer * spread : (peer + 1) * spread
            ]
    copies = [
        pltpu.make_async_copy(sent_ref.at[i], out_ref, sems.at[1 + i])
        for i, out_ref in enumerate(out_refs[1:])
    ]
    for copy in copies:
        copy.start()
    for copy in copies:
        copy.wait()


def swapped(value, flags):
    size = value.shape[0]
    for bit, flag in enumerate(flags):
        if flag is None:
            continue
        step = 1 << bit
        other = [value[start ^ step : (start ^ step) + step] for start in range(0, size, step)]
        value = jnp.where(flag, jnp.concatenate(other, axis=0), value)
    return value


def to_pairs(value, flags):
    half = value.shape[0] // 2
    value = swapped(value, flags)
    lines = [value[j * half + i : j * half + i + 1] for i in range(half) for j in range(2)]
    return jnp.concatenate(lines, axis=0)


def from_pairs(value, flags):
    size = value.shape[0]
    lines = [value[i : i + 1] for j in range(2) for i in range(j, size, 2)]
    return swapped(jnp.concatenate(lines, axis=0), flags)


def flags_of(pack_ref, shards, used):
    lines = pack_ref[2 * shards : 2 * shards + 8, :]
    return [lines[b : b + 1] > 0.5 if use else None for b, use in enumerate(used)]


def chunks_of(refs, parts, start):
    for i in range(0, len(refs), parts):
        yield refs[i : i + parts], start
        start += refs[i].shape[1]


def score_kernel(pack_ref, mixed_hbm, late_ref, *refs, used, parts):
    *early_refs, out_ref, late_mask_ref, early_mask_ref, mixed_ref, sems = refs
    arrivals = fetch(mixed_hbm, mixed_ref, sems)
    shards, rows = out_ref.shape
    spread = late_ref.shape[0] // shards
    late = late_ref.shape[1]
    late_mask = slot_mask(pack_ref[:shards, :], spread).astype(F32)
    early_mask = slot_mask(pack_ref[shards : 2 * shards, :], spread).astype(F32)
    late_mask_ref[...] = late_mask.reshape(late_mask_ref.shape).astype(BF16)
    early_mask_ref[...] = early_mask.reshape(early_mask_ref.shape).astype(BF16)
    flags = flags_of(pack_ref, shards, used)
    for copy in arrivals:
        copy.wait()

    def scored(rows_ref, mixed, mask):
        score = lax.dot_general(
            rows_ref[...], mixed, (((1,), (1,)), ((), ())), preferred_element_type=F32
        )
        score = (score[:, :rows] + score[:, rows:]).reshape(mask.shape)
        return jnp.sum(score * mask, axis=1)

    total = scored(late_ref, mixed_ref[:, :late], late_mask)
    for group, start in chunks_of(early_refs, parts, late):
        lines, each = [], shards // parts
        for i, early_ref in enumerate(group):
            mixed = mixed_ref[:, pl.ds(start, early_ref.shape[1])]
            lines.append(scored(early_ref, mixed, early_mask[i * each : (i + 1) * each]))
        total = total + from_pairs(jnp.concatenate(lines, axis=0), flags)
    out_ref[...] = total


def grad_kernel(
    own_ref, other_ref, pack_ref, late_mask_ref, early_mask_ref, late_ref, *refs, top, used, parts
):
    *early_refs, hidden_ref, out_ref, grad_ref = refs
    layers, rows, features = hidden_ref.shape
    shards = own_ref.shape[0]
    lines = grad_ref.shape[0]
    slots = 128 * ((out_ref.shape[1] - lines) // (2 * top))
    flags = flags_of(pack_ref, shards, used)
    pack = pack_ref[2 * shards + 8 :, :]
    shard, target = pack[:top], pack[top : 2 * top]
    weight, owner, column = [pack[2 * top + i : 2 * top + i + 1] for i in range(3)]
    inverse = pack[2 * top + 3 : 2 * top + 3 + layers]
    inverse = jnp.pad(inverse, ((0, 8 - layers), (0, 0))).T

    by_shard = own_ref[...] + other_ref[...]
    number = iota((shards, rows), 0).astype(F32)
    logits = jnp.concatenate(
        [
            jnp.sum(jnp.where(shard[k : k + 1] == number, by_shard, 0.0), axis=0, keepdims=True)
            for k in range(top)
        ],
        axis=0,
    )
    logits = logits - jnp.max(logits, axis=0, keepdims=True)
    logp = logits - jnp.log(jnp.sum(jnp.exp(logits), axis=0, keepdims=True))
    grad = weight * (jnp.exp(logp) - target)
    by_shard = jnp.zeros((shards, rows), F32)
    for k in range(top):
        by_shard = jnp.where(shard[k : k + 1] == number, grad[k : k + 1], by_shard)

    def spread_out(mask, values):
        mask = mask.astype(F32).reshape(values.shape[0], -1, rows)
        return (mask * values[:, None, :]).reshape(-1, rows).astype(BF16)

    late = late_ref.shape[1]
    pairs = to_pairs(by_shard, flags)
    part = spread_out(early_mask_ref[...], pairs)
    each = part.shape[0] // parts
    part = [part[i * each : (i + 1) * each] for i in range(parts)]
    sources = [([late_ref], [spread_out(late_mask_ref[...], by_shard)], 0)]
    for group, start in chunks_of(early_refs, parts, late):
        sources.append((group, part, start))
    for rows_refs, grads, start in sources:
        for cut in pieces(rows_refs[0].shape[1]):
            carried = sum(
                lax.dot_general(
                    grad, rows_ref[:, cut], (((0,), (0,)), ((), ())), preferred_element_type=F32
                )
                for rows_ref, grad in zip(rows_refs, grads)
            )
            wide, first = carried.shape[1], start + cut.start
            for layer in range(layers):
                scaled = hidden_ref[layer, :, pl.ds(first, wide)].astype(F32)
                scaled = scaled * inverse[:, layer : layer + 1]
                total = jnp.sum(scaled * carried, axis=0, keepdims=True)
                for j in range(wide // 128):
                    line = (layer * features + first) // 128 + j
                    grad_ref[line : line + 1, :] = total[:, j * 128 : (j + 1) * 128]

    high = logp.astype(BF16).astype(F32)
    halves = jnp.concatenate([high, logp - high], axis=0)
    owned = jnp.where(owner == iota((shards, 1, rows), 0).astype(F32), halves[None], 0.0)
    owned = owned.reshape(shards * 2 * top, rows).astype(BF16)
    placed = (iota((slots, rows), 0).astype(F32) == column).astype(BF16)
    sent = lax.dot_general(owned, placed, (((1,), (1,)), ((), ())), preferred_element_type=F32)
    sent = [
        sent[:, j * 128 : (j + 1) * 128].reshape(shards, 2 * top, 128) for j in range(slots // 128)
    ]
    out_ref[:, lines:, :] = jnp.concatenate(sent, axis=1).astype(BF16)
    grad = grad_ref[...].astype(BF16)
    for peer in range(shards):
        out_ref[peer, 0:lines, :] = grad


def sum_kernel(parts_ref, grad_ref, logp_ref):
    total = parts_ref[0].astype(F32)
    for peer in range(1, parts_ref.shape[0]):
        total = total + parts_ref[peer].astype(F32)
    layers, features = grad_ref.shape
    top, slots = logp_ref.shape
    each = features // 128
    for layer in range(layers):
        for j in range(each):
            line = layer * each + j
            grad_ref[layer : layer + 1, j * 128 : (j + 1) * 128] = total[line : line + 1]
    for j in range(slots // 128):
        first = layers * each + j * 2 * top
        logp_ref[:, j * 128 : (j + 1) * 128] = (
            total[first : first + top] + total[first + top : first + 2 * top]
        )


VMEM = pl.BlockSpec(memory_space=pltpu.VMEM)
HBM = pl.BlockSpec(memory_space=pltpu.HBM)


def params():
    return pltpu.CompilerParams(vmem_limit_bytes=VMEM_LIMIT)


def in_hbm(value):
    return pltpu.with_memory_space_constraint(value, pltpu.HBM)


def pick(asked, head, spread, late):
    rows = head.shape[0]
    slots, count = asked.shape[0] // 2 * spread, len(pieces(late))
    return pl.pallas_call(
        functools.partial(pick_kernel, spread=spread),
        in_specs=[VMEM, HBM],
        out_specs=HBM,
        out_shape=pltpu.HBM((slots, late), BF16),
        scratch_shapes=[
            pltpu.VMEM((rows, late), BF16),
            pltpu.VMEM((slots, late), BF16),
            pltpu.SemaphoreType.DMA((count,)),
            pltpu.SemaphoreType.DMA((count,)),
        ],
        compiler_params=params(),
        name="pick",
    )(asked, in_hbm(head))


def begin(group, shard, offset, head, peers, part, starts, wides):
    rows = shard.shape[1]
    return pl.pallas_call(
        functools.partial(begin_kernel, peers=peers, starts=starts),
        in_specs=[pl.BlockSpec(memory_space=pltpu.SMEM), HBM, HBM, HBM],
        out_specs=[HBM] + [VMEM] * len(wides),
        out_shape=[pltpu.HBM((2 * peers, rows), jnp.int32)]
        + [jax.ShapeDtypeStruct((part, wide), BF16) for wide in wides],
        scratch_shapes=[
            pltpu.VMEM(shard.shape, jnp.int32),
            pltpu.VMEM(shard.shape, jnp.int32),
            pltpu.VMEM((2 * peers, rows), jnp.int32),
            pltpu.SemaphoreType.DMA((3 + len(wides),)),
        ],
        compiler_params=params(),
        name="begin",
    )(group.reshape(1), in_hbm(shard), in_hbm(offset), in_hbm(head))


def pick_early(asked, head, near, far, spread, start, count):
    rows, wide = head.shape[0], near.shape[1]
    slots = asked.shape[0] * spread
    return pl.pallas_call(
        functools.partial(early_kernel, spread=spread, start=start),
        in_specs=[VMEM, HBM, VMEM, VMEM],
        out_specs=[VMEM] + [HBM] * (count - 1),
        out_shape=[jax.ShapeDtypeStruct((slots // count, wide), BF16)]
        + [pltpu.HBM((slots // count, wide), BF16)] * (count - 1),
        scratch_shapes=[
            pltpu.VMEM((rows, wide), BF16),
            pltpu.VMEM((max(1, count - 1), slots // count, wide), BF16),
            pltpu.SemaphoreType.DMA((count,)),
        ],
        compiler_params=params(),
        name="pick_early",
    )(asked, in_hbm(head), near, far)


def score(pack, mixed, late, early, shards, used, parts):
    rows = pack.shape[1]
    slots = sum(array.shape[0] for array in early[:parts])
    return pl.pallas_call(
        functools.partial(score_kernel, used=used, parts=parts),
        in_specs=[VMEM, HBM, VMEM] + [VMEM] * len(early),
        out_specs=[VMEM] * 3,
        out_shape=[
            jax.ShapeDtypeStruct((shards, rows), F32),
            jax.ShapeDtypeStruct((late.shape[0], rows), BF16),
            jax.ShapeDtypeStruct((slots, rows), BF16),
        ],
        scratch_shapes=[
            pltpu.VMEM(mixed.shape, BF16),
            pltpu.SemaphoreType.DMA((len(pieces(mixed.shape[1])),)),
        ],
        compiler_params=params(),
        name="score",
    )(pack, in_hbm(mixed), late, *early)


def gradient(own, other, pack, masks, late, early, hidden, lines, total_lines, top, used, parts):
    return pl.pallas_call(
        functools.partial(grad_kernel, top=top, used=used, parts=parts),
        in_specs=[VMEM] * (7 + len(early)),
        out_specs=VMEM,
        out_shape=jax.ShapeDtypeStruct((own.shape[0], total_lines, 128), BF16),
        scratch_shapes=[
            pltpu.VMEM((lines, 128), F32),
        ],
        compiler_params=params(),
        name="gradient",
    )(own, other, pack, *masks, late, *early, hidden)


def after(value, first):
    return lax.optimization_barrier((value, first))[0]


def add_up(parts, layers, features, top, slots):
    return pl.pallas_call(
        sum_kernel,
        in_specs=[VMEM],
        out_specs=[VMEM] * 2,
        out_shape=[
            jax.ShapeDtypeStruct((layers, features), F32),
            jax.ShapeDtypeStruct((top, slots), F32),
        ],
        compiler_params=params(),
        name="add_up",
    )(parts)


def rounded(value):
    return lax.reduce_precision(value, exponent_bits=8, mantissa_bits=7)


def position_weights(lengths, positions, sequences):
    seq_ends = jnp.cumsum(lengths)
    seq_starts = seq_ends - lengths
    position = jnp.arange(positions, dtype=jnp.int32)[None, :]
    member = (position >= seq_starts[:, None]) & (position < seq_ends[:, None])
    own_length = jnp.sum(jnp.where(member, lengths[:, None], 0), axis=0, keepdims=True)
    closing = jnp.any(member & (position == seq_ends[:, None] - 1), axis=0, keepdims=True)
    portion = 1.0 / (own_length.astype(F32) * sequences)
    return rounded(jnp.where(closing, 0.0, portion))


def swap_cores(value):
    size = lax.axis_size("mp")
    if size == 1:
        return jnp.zeros_like(value)
    return lax.ppermute(value, "mp", [(i, i ^ 1) for i in range(size)])


def exchange(value, groups=None):
    return lax.all_to_all(
        value, "dp", split_axis=0, concat_axis=0, tiled=True, axis_index_groups=groups
    )


def local(
    hidden,
    row_owner,
    candidate_shard,
    candidate_offset,
    target_logits,
    lengths,
    layer_mix,
    draft_head,
):
    rows, layers, features = hidden.shape
    top = candidate_shard.shape[1]
    peers = lax.axis_size("dp")
    cores = lax.axis_size("mp")
    capacity = max(2, 2 * rows // peers)
    spread = min(rows, max(2, 3 * rows * top // (2 * peers)))
    spread = -(-spread // 16) * 16
    half = peers // 2
    late = features - sum(CHUNKS) * features // 2048
    place, group = lax.axis_index("dp"), lax.axis_index("groups")

    count = draft_head.shape[0]
    part = count // 2
    wides = [wide * features // 2048 for wide in CHUNKS]
    starts = [late + sum(wides[:i]) for i in range(len(wides))]
    shard, offset = candidate_shard.T, candidate_offset.T
    message, *slices = begin(group, shard, offset, draft_head, peers, part, starts, wides)
    across = [(i, (i + half) % peers) for i in range(peers)]
    chunks = [(start, lax.ppermute(near, "dp", across)) for start, near in zip(starts, slices)]
    wanted = exchange(message.reshape(peers, 2, rows)).reshape(2 * peers, rows)

    picked = pick(wanted, draft_head, spread, late)
    rows_late = exchange(picked.reshape(peers, spread, late)).reshape(peers * spread, late)

    few = half <= 4
    parts = half if few else 1
    bits = [b for b in range(peers.bit_length() - 1) if few or 1 << b == half]
    used = [b in bits for b in range(peers.bit_length() - 1)]
    flags = [(place >> b) & 1 if use else None for b, use in enumerate(used)]
    wanted = lax.dynamic_slice(wanted, (place // half * half * 2, 0), (half * 2, rows))
    wanted = swapped(wanted, [None] + [None if flag is None else flag > 0 for flag in flags[:-1]])
    rows_early = []
    for start, near in chunks:
        near = after(near, picked)
        far = lax.ppermute(near, "groups", [(0, 1), (1, 0)])
        rows_here = list(pick_early(wanted, draft_head, near, far, spread, start, parts))
        if few:
            for i in reversed(range(1, half)):
                rows_here[i] = lax.ppermute(rows_here[i], "dp", [(j, j ^ i) for j in range(peers)])
        else:
            halves = [list(range(half)), list(range(half, peers))]
            rows_here = exchange(rows_here[0].reshape(half, 2 * spread, -1), halves)
            rows_here = [rows_here.reshape(peers * spread, -1)]
        rows_early += rows_here

    number = jnp.arange(peers, dtype=jnp.int32)[:, None]
    asked = jnp.max(
        jnp.where(shard[:, None, :] == number[None], offset[:, None, :], -1), axis=0
    )
    tokens = hidden.transpose(1, 0, 2)
    wide = tokens.astype(F32)
    squares = jnp.sum(wide * wide, axis=2)
    squares = squares + swap_cores(squares)
    inverse = lax.rsqrt(squares / (features * cores) + EPS)
    mixed = jnp.sum(wide * layer_mix[:, None, :] * inverse[:, :, None], axis=0)
    high = rounded(mixed)
    mixed = jnp.concatenate([high, mixed - high], axis=0).astype(BF16)

    weight = position_weights(lengths[0], rows, float(lengths.shape[1] * peers))
    target = jax.nn.softmax(target_logits.T.astype(F32), axis=0)
    owner = row_owner.T
    same = (owner.T == owner) & (iota((rows, rows), 1) < iota((rows, rows), 0))
    column = lax.axis_index("dp") * capacity + jnp.sum(same.astype(jnp.int32), axis=1)[None, :]
    held = [jnp.full((1, rows), 0 if flag is None else flag, jnp.int32) for flag in flags]
    held = jnp.pad(jnp.concatenate(held, axis=0), ((0, 8 - len(held)), (0, 0)))
    pairs = to_pairs(asked, [None if flag is None else flag > 0 for flag in flags])
    pack = [asked, pairs, held, shard, target, weight, owner, column, inverse]
    pack = jnp.concatenate([value.astype(F32) for value in pack], axis=0)
    pack = jnp.pad(pack, ((0, -pack.shape[0] % 8), (0, 0)))

    slots = peers * capacity
    lines = layers * features // 128
    total_lines = lines + 2 * top * slots // 128
    own, *masks = score(pack, mixed, rows_late, rows_early, peers, used, parts)
    other = swap_cores(own)
    sent = gradient(
        own, other, pack, masks, rows_late, rows_early, tokens, lines, total_lines, top, used, parts
    )
    grad, logp = add_up(exchange(sent), layers, features, top, slots)
    return (logp.T[None], grad)


def solution(mesh):
    return jax.shard_map(
        local,
        mesh=mesh,
        in_specs=(
            P(("groups", "dp"), None, "mp"),
            P(("groups", "dp"), None),
            P(("groups", "dp"), None),
            P(("groups", "dp"), None),
            P(("groups", "dp"), None),
            P(("groups", "dp"), None),
            P(None, "mp"),
            P("dp", "mp"),
        ),
        out_specs=(P(("groups", "dp"), None, None), P("groups", "mp")),
        check_vma=False,
    )
```

```python
import functools

import jax
import jax.numpy as jnp
from jax import lax
from jax.experimental import pallas as pl
from jax.experimental.pallas import tpu as pltpu
from jax.sharding import PartitionSpec as P

EPS = 1e-06
HIGHEST = lax.Precision.HIGHEST
F32 = jnp.float32
BF16 = jnp.bfloat16
VMEM_LIMIT = 16 * 1024 * 1024
CHUNKS = (128, 512)


def iota(shape, axis):
    return lax.broadcasted_iota(jnp.int32, shape, axis)


def slot_mask(asked, spread):
    shards, rows = asked.shape
    held = asked >= 0
    earlier = (iota((rows, rows), 0) < iota((rows, rows), 1)).astype(BF16)
    rank = jnp.dot(held.astype(BF16), earlier, preferred_element_type=F32)
    rank = jnp.where(held, rank, -1.0)
    place = iota((shards, spread, rows), 1).astype(F32)
    return rank[:, None, :] == place


def pieces(features):
    return [pl.ds(start, min(512, features - start)) for start in range(0, features, 512)]


def fetch(source, target, sems):
    lead = (slice(None),) * (len(source.shape) - 1)
    copies = [
        pltpu.make_async_copy(source.at[(*lead, cut)], target.at[(*lead, cut)], sems.at[i])
        for i, cut in enumerate(pieces(source.shape[-1]))
    ]
    for copy in copies:
        copy.start()
    return copies


def hot_rows(asked, spread, count):
    shards, rows = asked.shape
    mask = slot_mask(asked, spread)
    row = jnp.where(mask, (asked.astype(F32) + 1.0)[:, None, :], 0.0)
    row = jnp.sum(row.reshape(shards * spread, rows), axis=1, keepdims=True) - 1.0
    return jnp.where(row == iota((1, count), 1).astype(F32), 1.0, 0.0).astype(BF16)


def every_other(ref, first):
    lines = [ref[i : i + 1, :] for i in range(first, ref.shape[0], 2)]
    return jnp.concatenate(lines, axis=0)


def pick_kernel(asked_ref, head_hbm, out_hbm, head_ref, picked_ref, in_sems, out_sems, *, spread):
    late = head_ref.shape[1]
    arrivals = fetch(head_hbm.at[:, :late], head_ref, in_sems)
    hot = hot_rows(every_other(asked_ref, 0), spread, head_ref.shape[0])
    departures = []
    for i, cut in enumerate(pieces(late)):
        arrivals[i].wait()
        picked_ref[:, cut] = jnp.dot(
            hot, head_ref[:, cut], preferred_element_type=F32
        ).astype(BF16)
        copy = pltpu.make_async_copy(picked_ref.at[:, cut], out_hbm.at[:, cut], out_sems.at[i])
        copy.start()
        departures.append(copy)
    for copy in departures:
        copy.wait()


def begin_kernel(
    group_ref, shard_hbm, offset_hbm, head_hbm, message_hbm, *refs, peers, starts
):
    *out_refs, shard_ref, offset_ref, message_ref, sems = refs
    small = [
        pltpu.make_async_copy(shard_hbm, shard_ref, sems.at[0]),
        pltpu.make_async_copy(offset_hbm, offset_ref, sems.at[1]),
    ]
    large = []
    part = out_refs[0].shape[0]
    shift = group_ref[0] * part
    for i, out_ref in enumerate(out_refs):
        rows = pl.ds(pl.multiple_of(shift, part), part)
        source = head_hbm.at[rows, pl.ds(starts[i], out_ref.shape[1])]
        large.append(pltpu.make_async_copy(source, out_ref, sems.at[3 + i]))
    for copy in small + large:
        copy.start()
    for copy in small:
        copy.wait()
    shard, offset = shard_ref[...], offset_ref[...]
    count = head_hbm.shape[0]
    other = offset + shift
    other = jnp.where(other >= count, other - count, other)
    line = iota(message_ref.shape, 0)
    number = line // 2 + jnp.where(line % 2 == 0, 0, peers // 2)
    number = jnp.where(number >= peers, number - peers, number)
    message = jnp.full(message_ref.shape, -1, jnp.int32)
    for k in range(shard.shape[0]):
        asked = jnp.where(line % 2 == 0, offset[k : k + 1], other[k : k + 1])
        message = jnp.where(shard[k : k + 1] == number, asked, message)
    message_ref[...] = message
    copy = pltpu.make_async_copy(message_ref, message_hbm, sems.at[2])
    copy.start()
    copy.wait()
    for copy in large:
        copy.wait()


def early_kernel(asked_ref, head_hbm, near_ref, far_ref, *refs, spread, start):
    *out_refs, own_ref, sent_ref, sems = refs
    count, wide = own_ref.shape
    copy = pltpu.make_async_copy(head_hbm.at[:, pl.ds(start, wide)], own_ref, sems.at[0])
    copy.start()
    peers = asked_ref.shape[0] // 2
    hot = [hot_rows(every_other(asked_ref, i), spread, count) for i in range(2)]
    other = sum(
        jnp.dot(
            hot[1][:, j * count // 2 : (j + 1) * count // 2],
            ref[...],
            preferred_element_type=F32,
        )
        for j, ref in enumerate((near_ref, far_ref))
    )
    copy.wait()
    own = jnp.dot(hot[0], own_ref[...], preferred_element_type=F32)
    each = 2 * peers * spread // len(out_refs)
    targets = [out_refs[0]] + [sent_ref.at[i] for i in range(len(out_refs) - 1)]
    for i, picked in enumerate((own.astype(BF16), other.astype(BF16))):
        for peer in range(peers):
            first = (2 * peer + i) * spread
            targets[first // each][first % each : first % each + spread, :] = picked[
                peer * spread : (peer + 1) * spread
            ]
    copies = [
        pltpu.make_async_copy(sent_ref.at[i], out_ref, sems.at[1 + i])
        for i, out_ref in enumerate(out_refs[1:])
    ]
    for copy in copies:
        copy.start()
    for copy in copies:
        copy.wait()


def swapped(value, flags):
    size = value.shape[0]
    for bit, flag in enumerate(flags):
        if flag is None:
            continue
        step = 1 << bit
        other = [value[start ^ step : (start ^ step) + step] for start in range(0, size, step)]
        value = jnp.where(flag, jnp.concatenate(other, axis=0), value)
    return value


def to_pairs(value, flags):
    half = value.shape[0] // 2
    value = swapped(value, flags)
    lines = [value[j * half + i : j * half + i + 1] for i in range(half) for j in range(2)]
    return jnp.concatenate(lines, axis=0)


def from_pairs(value, flags):
    size = value.shape[0]
    lines = [value[i : i + 1] for j in range(2) for i in range(j, size, 2)]
    return swapped(jnp.concatenate(lines, axis=0), flags)


def flags_of(pack_ref, shards, used):
    lines = pack_ref[2 * shards : 2 * shards + 8, :]
    return [lines[b : b + 1] > 0.5 if use else None for b, use in enumerate(used)]


def chunks_of(refs, parts, start):
    for i in range(0, len(refs), parts):
        yield refs[i : i + parts], start
        start += refs[i].shape[1]


def score_kernel(pack_ref, mixed_hbm, late_ref, *refs, used, parts):
    *early_refs, out_ref, late_mask_ref, early_mask_ref, mixed_ref, sems = refs
    arrivals = fetch(mixed_hbm, mixed_ref, sems)
    shards, rows = out_ref.shape
    spread = late_ref.shape[0] // shards
    late = late_ref.shape[1]
    late_mask = slot_mask(pack_ref[:shards, :], spread).astype(F32)
    early_mask = slot_mask(pack_ref[shards : 2 * shards, :], spread).astype(F32)
    late_mask_ref[...] = late_mask.reshape(late_mask_ref.shape).astype(BF16)
    early_mask_ref[...] = early_mask.reshape(early_mask_ref.shape).astype(BF16)
    flags = flags_of(pack_ref, shards, used)
    for copy in arrivals:
        copy.wait()

    def scored(rows_ref, mixed, mask):
        score = lax.dot_general(
            rows_ref[...], mixed, (((1,), (1,)), ((), ())), preferred_element_type=F32
        )
        score = (score[:, :rows] + score[:, rows:]).reshape(mask.shape)
        return jnp.sum(score * mask, axis=1)

    total = scored(late_ref, mixed_ref[:, :late], late_mask)
    for group, start in chunks_of(early_refs, parts, late):
        lines, each = [], shards // parts
        for i, early_ref in enumerate(group):
            mixed = mixed_ref[:, pl.ds(start, early_ref.shape[1])]
            lines.append(scored(early_ref, mixed, early_mask[i * each : (i + 1) * each]))
        total = total + from_pairs(jnp.concatenate(lines, axis=0), flags)
    out_ref[...] = total


def grad_kernel(
    own_ref, other_ref, pack_ref, late_mask_ref, early_mask_ref, late_ref, *refs, top, used, parts
):
    *early_refs, hidden_ref, out_ref, grad_ref = refs
    layers, rows, features = hidden_ref.shape
    shards = own_ref.shape[0]
    lines = grad_ref.shape[0]
    slots = 128 * ((out_ref.shape[1] - lines) // (2 * top))
    flags = flags_of(pack_ref, shards, used)
    pack = pack_ref[2 * shards + 8 :, :]
    shard, target = pack[:top], pack[top : 2 * top]
    weight, owner, column = [pack[2 * top + i : 2 * top + i + 1] for i in range(3)]
    inverse = pack[2 * top + 3 : 2 * top + 3 + layers]
    inverse = jnp.pad(inverse, ((0, 8 - layers), (0, 0))).T

    by_shard = own_ref[...] + other_ref[...]
    number = iota((shards, rows), 0).astype(F32)
    logits = jnp.concatenate(
        [
            jnp.sum(jnp.where(shard[k : k + 1] == number, by_shard, 0.0), axis=0, keepdims=True)
            for k in range(top)
        ],
        axis=0,
    )
    logits = logits - jnp.max(logits, axis=0, keepdims=True)
    logp = logits - jnp.log(jnp.sum(jnp.exp(logits), axis=0, keepdims=True))
    grad = weight * (jnp.exp(logp) - target)
    by_shard = jnp.zeros((shards, rows), F32)
    for k in range(top):
        by_shard = jnp.where(shard[k : k + 1] == number, grad[k : k + 1], by_shard)

    def spread_out(mask, values):
        mask = mask.astype(F32).reshape(values.shape[0], -1, rows)
        return (mask * values[:, None, :]).reshape(-1, rows).astype(BF16)

    late = late_ref.shape[1]
    pairs = to_pairs(by_shard, flags)
    part = spread_out(early_mask_ref[...], pairs)
    each = part.shape[0] // parts
    part = [part[i * each : (i + 1) * each] for i in range(parts)]
    sources = [([late_ref], [spread_out(late_mask_ref[...], by_shard)], 0)]
    for group, start in chunks_of(early_refs, parts, late):
        sources.append((group, part, start))
    for rows_refs, grads, start in sources:
        for cut in pieces(rows_refs[0].shape[1]):
            carried = sum(
                lax.dot_general(
                    grad, rows_ref[:, cut], (((0,), (0,)), ((), ())), preferred_element_type=F32
                )
                for rows_ref, grad in zip(rows_refs, grads)
            )
            wide, first = carried.shape[1], start + cut.start
            for layer in range(layers):
                scaled = hidden_ref[layer, :, pl.ds(first, wide)].astype(F32)
                scaled = scaled * inverse[:, layer : layer + 1]
                total = jnp.sum(scaled * carried, axis=0, keepdims=True)
                for j in range(wide // 128):
                    line = (layer * features + first) // 128 + j
                    grad_ref[line : line + 1, :] = total[:, j * 128 : (j + 1) * 128]

    high = logp.astype(BF16).astype(F32)
    halves = jnp.concatenate([high, logp - high], axis=0)
    owned = jnp.where(owner == iota((shards, 1, rows), 0).astype(F32), halves[None], 0.0)
    owned = owned.reshape(shards * 2 * top, rows).astype(BF16)
    placed = (iota((slots, rows), 0).astype(F32) == column).astype(BF16)
    sent = lax.dot_general(owned, placed, (((1,), (1,)), ((), ())), preferred_element_type=F32)
    sent = [
        sent[:, j * 128 : (j + 1) * 128].reshape(shards, 2 * top, 128) for j in range(slots // 128)
    ]
    out_ref[:, lines:, :] = jnp.concatenate(sent, axis=1).astype(BF16)
    grad = grad_ref[...].astype(BF16)
    for peer in range(shards):
        out_ref[peer, 0:lines, :] = grad


def sum_kernel(parts_ref, grad_ref, logp_ref):
    total = parts_ref[0].astype(F32)
    for peer in range(1, parts_ref.shape[0]):
        total = total + parts_ref[peer].astype(F32)
    layers, features = grad_ref.shape
    top, slots = logp_ref.shape
    each = features // 128
    for layer in range(layers):
        for j in range(each):
            line = layer * each + j
            grad_ref[layer : layer + 1, j * 128 : (j + 1) * 128] = total[line : line + 1]
    for j in range(slots // 128):
        first = layers * each + j * 2 * top
        logp_ref[:, j * 128 : (j + 1) * 128] = (
            total[first : first + top] + total[first + top : first + 2 * top]
        )


VMEM = pl.BlockSpec(memory_space=pltpu.VMEM)
HBM = pl.BlockSpec(memory_space=pltpu.HBM)


def params():
    return pltpu.CompilerParams(vmem_limit_bytes=VMEM_LIMIT)


def in_hbm(value):
    return pltpu.with_memory_space_constraint(value, pltpu.HBM)


def pick(asked, head, spread, late):
    rows = head.shape[0]
    slots, count = asked.shape[0] // 2 * spread, len(pieces(late))
    return pl.pallas_call(
        functools.partial(pick_kernel, spread=spread),
        in_specs=[VMEM, HBM],
        out_specs=HBM,
        out_shape=pltpu.HBM((slots, late), BF16),
        scratch_shapes=[
            pltpu.VMEM((rows, late), BF16),
            pltpu.VMEM((slots, late), BF16),
            pltpu.SemaphoreType.DMA((count,)),
            pltpu.SemaphoreType.DMA((count,)),
        ],
        compiler_params=params(),
        name="pick",
    )(asked, in_hbm(head))


def begin(group, shard, offset, head, peers, part, starts, wides):
    rows = shard.shape[1]
    return pl.pallas_call(
        functools.partial(begin_kernel, peers=peers, starts=starts),
        in_specs=[pl.BlockSpec(memory_space=pltpu.SMEM), HBM, HBM, HBM],
        out_specs=[HBM] + [VMEM] * len(wides),
        out_shape=[pltpu.HBM((2 * peers, rows), jnp.int32)]
        + [jax.ShapeDtypeStruct((part, wide), BF16) for wide in wides],
        scratch_shapes=[
            pltpu.VMEM(shard.shape, jnp.int32),
            pltpu.VMEM(shard.shape, jnp.int32),
            pltpu.VMEM((2 * peers, rows), jnp.int32),
            pltpu.SemaphoreType.DMA((3 + len(wides),)),
        ],
        compiler_params=params(),
        name="begin",
    )(group.reshape(1), in_hbm(shard), in_hbm(offset), in_hbm(head))


def pick_early(asked, head, near, far, spread, start, count):
    rows, wide = head.shape[0], near.shape[1]
    slots = asked.shape[0] * spread
    return pl.pallas_call(
        functools.partial(early_kernel, spread=spread, start=start),
        in_specs=[VMEM, HBM, VMEM, VMEM],
        out_specs=[VMEM] + [HBM] * (count - 1),
        out_shape=[jax.ShapeDtypeStruct((slots // count, wide), BF16)]
        + [pltpu.HBM((slots // count, wide), BF16)] * (count - 1),
        scratch_shapes=[
            pltpu.VMEM((rows, wide), BF16),
            pltpu.VMEM((max(1, count - 1), slots // count, wide), BF16),
            pltpu.SemaphoreType.DMA((count,)),
        ],
        compiler_params=params(),
        name="pick_early",
    )(asked, in_hbm(head), near, far)


def score(pack, mixed, late, early, shards, used, parts):
    rows = pack.shape[1]
    slots = sum(array.shape[0] for array in early[:parts])
    return pl.pallas_call(
        functools.partial(score_kernel, used=used, parts=parts),
        in_specs=[VMEM, HBM, VMEM] + [VMEM] * len(early),
        out_specs=[VMEM] * 3,
        out_shape=[
            jax.ShapeDtypeStruct((shards, rows), F32),
            jax.ShapeDtypeStruct((late.shape[0], rows), BF16),
            jax.ShapeDtypeStruct((slots, rows), BF16),
        ],
        scratch_shapes=[
            pltpu.VMEM(mixed.shape, BF16),
            pltpu.SemaphoreType.DMA((len(pieces(mixed.shape[1])),)),
        ],
        compiler_params=params(),
        name="score",
    )(pack, in_hbm(mixed), late, *early)


def gradient(own, other, pack, masks, late, early, hidden, lines, total_lines, top, used, parts):
    return pl.pallas_call(
        functools.partial(grad_kernel, top=top, used=used, parts=parts),
        in_specs=[VMEM] * (7 + len(early)),
        out_specs=VMEM,
        out_shape=jax.ShapeDtypeStruct((own.shape[0], total_lines, 128), BF16),
        scratch_shapes=[
            pltpu.VMEM((lines, 128), F32),
        ],
        compiler_params=params(),
        name="gradient",
    )(own, other, pack, *masks, late, *early, hidden)


def after(value, first):
    return lax.optimization_barrier((value, first))[0]


def add_up(parts, layers, features, top, slots):
    return pl.pallas_call(
        sum_kernel,
        in_specs=[VMEM],
        out_specs=[VMEM] * 2,
        out_shape=[
            jax.ShapeDtypeStruct((layers, features), F32),
            jax.ShapeDtypeStruct((top, slots), F32),
        ],
        compiler_params=params(),
        name="add_up",
    )(parts)


def rounded(value):
    return lax.reduce_precision(value, exponent_bits=8, mantissa_bits=7)


def position_weights(lengths, positions, sequences):
    seq_ends = jnp.cumsum(lengths)
    seq_starts = seq_ends - lengths
    position = jnp.arange(positions, dtype=jnp.int32)[None, :]
    member = (position >= seq_starts[:, None]) & (position < seq_ends[:, None])
    own_length = jnp.sum(jnp.where(member, lengths[:, None], 0), axis=0, keepdims=True)
    closing = jnp.any(member & (position == seq_ends[:, None] - 1), axis=0, keepdims=True)
    portion = 1.0 / (own_length.astype(F32) * sequences)
    return rounded(jnp.where(closing, 0.0, portion))


def swap_cores(value):
    size = lax.axis_size("mp")
    if size == 1:
        return jnp.zeros_like(value)
    return lax.ppermute(value, "mp", [(i, i ^ 1) for i in range(size)])


def exchange(value, groups=None):
    return lax.all_to_all(
        value, "dp", split_axis=0, concat_axis=0, tiled=True, axis_index_groups=groups
    )


def local(
    hidden,
    row_owner,
    candidate_shard,
    candidate_offset,
    target_logits,
    lengths,
    layer_mix,
    draft_head,
):
    rows, layers, features = hidden.shape
    top = candidate_shard.shape[1]
    peers = lax.axis_size("dp")
    cores = lax.axis_size("mp")
    capacity = max(2, 2 * rows // peers)
    spread = min(rows, max(2, 3 * rows * top // (2 * peers)))
    spread = -(-spread // 16) * 16
    half = peers // 2
    late = features - sum(CHUNKS) * features // 2048
    place, group = lax.axis_index("dp"), lax.axis_index("groups")

    count = draft_head.shape[0]
    part = count // 2
    wides = [wide * features // 2048 for wide in CHUNKS]
    starts = [late + sum(wides[:i]) for i in range(len(wides))]
    shard, offset = candidate_shard.T, candidate_offset.T
    message, *slices = begin(group, shard, offset, draft_head, peers, part, starts, wides)
    across = [(i, (i + half) % peers) for i in range(peers)]
    chunks = [(start, lax.ppermute(near, "dp", across)) for start, near in zip(starts, slices)]
    wanted = exchange(message.reshape(peers, 2, rows)).reshape(2 * peers, rows)

    picked = pick(wanted, draft_head, spread, late)
    rows_late = exchange(picked.reshape(peers, spread, late)).reshape(peers * spread, late)

    few = half <= 4
    parts = half if few else 1
    bits = [b for b in range(peers.bit_length() - 1) if few or 1 << b == half]
    used = [b in bits for b in range(peers.bit_length() - 1)]
    flags = [(place >> b) & 1 if use else None for b, use in enumerate(used)]
    wanted = lax.dynamic_slice(wanted, (place // half * half * 2, 0), (half * 2, rows))
    wanted = swapped(wanted, [None] + [None if flag is None else flag > 0 for flag in flags[:-1]])
    rows_early = []
    for start, near in chunks:
        near = after(near, picked)
        far = lax.ppermute(near, "groups", [(0, 1), (1, 0)])
        rows_here = list(pick_early(wanted, draft_head, near, far, spread, start, parts))
        if few:
            for i in range(1, half):
                rows_here[i] = lax.ppermute(rows_here[i], "dp", [(j, j ^ i) for j in range(peers)])
        else:
            halves = [list(range(half)), list(range(half, peers))]
            rows_here = exchange(rows_here[0].reshape(half, 2 * spread, -1), halves)
            rows_here = [rows_here.reshape(peers * spread, -1)]
        rows_early += rows_here

    number = jnp.arange(peers, dtype=jnp.int32)[:, None]
    asked = jnp.max(
        jnp.where(shard[:, None, :] == number[None], offset[:, None, :], -1), axis=0
    )
    tokens = hidden.transpose(1, 0, 2)
    wide = tokens.astype(F32)
    squares = jnp.sum(wide * wide, axis=2)
    squares = squares + swap_cores(squares)
    inverse = lax.rsqrt(squares / (features * cores) + EPS)
    mixed = jnp.sum(wide * layer_mix[:, None, :] * inverse[:, :, None], axis=0)
    high = rounded(mixed)
    mixed = jnp.concatenate([high, mixed - high], axis=0).astype(BF16)

    weight = position_weights(lengths[0], rows, float(lengths.shape[1] * peers))
    target = jax.nn.softmax(target_logits.T.astype(F32), axis=0)
    owner = row_owner.T
    same = (owner.T == owner) & (iota((rows, rows), 1) < iota((rows, rows), 0))
    column = lax.axis_index("dp") * capacity + jnp.sum(same.astype(jnp.int32), axis=1)[None, :]
    held = [jnp.full((1, rows), 0 if flag is None else flag, jnp.int32) for flag in flags]
    held = jnp.pad(jnp.concatenate(held, axis=0), ((0, 8 - len(held)), (0, 0)))
    pairs = to_pairs(asked, [None if flag is None else flag > 0 for flag in flags])
    pack = [asked, pairs, held, shard, target, weight, owner, column, inverse]
    pack = jnp.concatenate([value.astype(F32) for value in pack], axis=0)
    pack = jnp.pad(pack, ((0, -pack.shape[0] % 8), (0, 0)))

    slots = peers * capacity
    lines = layers * features // 128
    total_lines = lines + 2 * top * slots // 128
    own, *masks = score(pack, mixed, rows_late, rows_early, peers, used, parts)
    other = swap_cores(own)
    sent = gradient(
        own, other, pack, masks, rows_late, rows_early, tokens, lines, total_lines, top, used, parts
    )
    grad, logp = add_up(exchange(sent), layers, features, top, slots)
    return (logp.T[None], grad)


def solution(mesh):
    return jax.shard_map(
        local,
        mesh=mesh,
        in_specs=(
            P(("groups", "dp"), None, "mp"),
            P(("groups", "dp"), None),
            P(("groups", "dp"), None),
            P(("groups", "dp"), None),
            P(("groups", "dp"), None),
            P(("groups", "dp"), None),
            P(None, "mp"),
            P("dp", "mp"),
        ),
        out_specs=(P(("groups", "dp"), None, None), P("groups", "mp")),
        check_vma=False,
    )
```
